32 devices in a mesh: node: 4 (over z), local: 4 (over y, x), cuts: 2 (over core).
Axes of the slice: x: 2, y: 2, z: 4, core: 2. Of those that a mesh axis runs over, the one named last changes fastest.
Arguments:
- tokens: bfloat16 [384, 3584], P('node', 'cuts'), may hold values from -6 to 6
- expert_ids: int32 [384, 8], P('node'), may hold values from 0 to 7, as said below
- affinity: float32 [384, 8], P('node'), may hold values from 0.1 to 1
- w_gate: bfloat16 [16, 3584, 512], P(('node', 'local'), 'cuts'), may hold values from -0.09375 to 0.09375
- w_up: bfloat16 [16, 3584, 512], P(('node', 'local'), 'cuts'), may hold values from -0.09375 to 0.09375
- w_down: bfloat16 [16, 512, 3584], P(('node', 'local'), None, 'cuts'), may hold values from -0.1875 to 0.1875
Outputs:
- moe_out: bfloat16 [384, 3584], P(('node', 'local'), 'cuts')
The draws below stay inside these ranges and needn't reach their ends.
Inputs may be any that keep to these rules, and one draw needn't show every extreme that they name: `expert_ids`: each row names both experts 2m and 2m + 1 of each of 4 different nodes m, in some order.
All inputs are finite; a program needn't handle non-finite values.
Results may differ from the reference program's by a relative error of at most 0.009.
Values may be sent and summed in bfloat16 or wider, within the bound.
No kernel may reach another device: no remote copies, remote signals or barrier semaphores. Data moves between devices by JAX's collectives and lax.ppermute only.
A program may use at most 64 MiB of HBM per device.

```python
import jax
import jax.numpy as jnp
from jax import lax

D = 3584
FF = 1024
TOPK = 8
NODE_LIMIT = 4
TOK_NODE = 96
EXPERTS = 8
GROUP = 2
HID = 512
SHARDS = 16
CAP = 120
TOKENS = 384
N_NODE = 4


def draw_expert_ids(key, part):
    key_pop = jax.random.fold_in(key, 11)
    key_noise = jax.random.fold_in(key, 12)
    key_order = jax.random.fold_in(key, 13)
    node_count = EXPERTS // 2
    popular = jax.random.randint(key_pop, (node_count,), 0, 600)
    noise = jax.random.randint(key_noise, (TOKENS, node_count), 0, 1000)
    scores = (noise + popular[None, :]) * node_count + jnp.arange(node_count, dtype=jnp.int32)[None, :]
    _, chosen = lax.top_k(scores, NODE_LIMIT)
    paired = jnp.stack([2 * chosen, 2 * chosen + 1], axis=-1).reshape(TOKENS, TOPK)
    order_keys = jax.random.randint(key_order, (TOKENS, TOPK), 0, 1 << 20) * TOPK + jnp.arange(TOPK, dtype=jnp.int32)[None, :]
    order = jnp.argsort(order_keys, axis=1, stable=True)
    return jnp.take_along_axis(paired, order, axis=1).astype(jnp.int32)


def steps_of(stream_key, dims, pieces, smallest, high):
    loudness, own = 1.0, jax.random.fold_in(stream_key, 6)
    for dim, blocks in pieces:
        draws = jnp.exp(jax.random.uniform(jax.random.fold_in(own, dim), (blocks,), jnp.float32, smallest / len(pieces), high / len(pieces)))
        loudness = loudness * jnp.repeat(draws, dims[dim] // blocks).reshape([-1 if axis == dim else 1 for axis in range(len(dims))])
    return loudness


def scatter_about(stream_key, dims, deviation, bound, shards=(), kind=jnp.bfloat16):
    gain = steps_of(stream_key, dims, shards, -0.22, 0.18) if shards else 1.0
    drawn = jax.random.normal(stream_key, dims, jnp.float32) * deviation * gain
    return jnp.minimum(jnp.maximum(drawn, -bound), bound).astype(kind)


def setup_inputs(seed: int = 0) -> dict:
    keys = jax.random.split(jax.random.key(seed), 7)
    return {
        "tokens": scatter_about(keys[0], (TOKENS, D), 1.0, 6.0, ((0, 4), (1, 2))),
        "expert_ids": draw_expert_ids(jax.random.fold_in(keys[6], 71), 0),
        "affinity": jnp.clip(0.1 + 0.9 * jax.random.uniform(keys[2], (TOKENS, TOPK), jnp.float32) ** steps_of(keys[2], (TOKENS, TOPK), ((0, 4),), -0.2, 0.2), 0.1, 1.0),
        "w_gate": scatter_about(keys[3], (SHARDS, D, HID), D ** -0.5, 0.09375, ((0, 16), (1, 2))),
        "w_up": scatter_about(keys[4], (SHARDS, D, HID), D ** -0.5, 0.09375, ((0, 16), (1, 2))),
        "w_down": scatter_about(keys[5], (SHARDS, HID, D), FF ** -0.5, 0.1875, ((0, 16), (2, 2))),
    }


def reference(tokens, expert_ids, affinity, w_gate, w_up, w_down):
    expert_range = jnp.arange(EXPERTS, dtype=jnp.int32)
    route_hit = (expert_ids[:, :, None] == expert_range[None, None, :]).astype(jnp.int32)
    member = jnp.sum(route_hit, axis=1)
    blocked = member.reshape(N_NODE, TOK_NODE, EXPERTS)
    block_rank = (jnp.cumsum(blocked, axis=1) - blocked).reshape(TOKENS, EXPERTS)
    kept_mask = (member > 0) & (block_rank < CAP)
    affinity_sum = jnp.sum(affinity, axis=1, keepdims=True)
    weight = (2.5 * affinity / affinity_sum).astype(jnp.bfloat16).astype(jnp.float32)
    route_weight = jnp.sum(route_hit.astype(jnp.float32) * weight[:, :, None], axis=1)
    source = jnp.arange(TOKENS, dtype=jnp.int32) // TOK_NODE
    position = (source[:, None] * CAP + block_rank).astype(jnp.int32)
    row_count = N_NODE * CAP
    token_range = jnp.arange(TOKENS, dtype=jnp.int32)

    def one_expert(accumulated, expert_index):
        target = jnp.where(kept_mask[:, expert_index], position[:, expert_index], row_count).astype(jnp.int32)
        owner_token = jnp.full((row_count + 1,), TOKENS, jnp.int32).at[target].set(token_range)[:row_count]
        filled = owner_token < TOKENS
        safe_token = jnp.minimum(owner_token, TOKENS - 1).astype(jnp.int32)
        expert_rows = jnp.where(filled[:, None], tokens[safe_token], jnp.zeros((), tokens.dtype))
        start = (expert_index * GROUP).astype(jnp.int32)
        gate_slices = lax.dynamic_slice_in_dim(w_gate, start, GROUP, 0)
        up_slices = lax.dynamic_slice_in_dim(w_up, start, GROUP, 0)
        down_slices = lax.dynamic_slice_in_dim(w_down, start, GROUP, 0)
        gate_full = jnp.transpose(gate_slices, (1, 0, 2)).reshape(D, FF)
        up_full = jnp.transpose(up_slices, (1, 0, 2)).reshape(D, FF)
        gate_value = jnp.dot(expert_rows, gate_full, preferred_element_type=jnp.float32)
        up_value = jnp.dot(expert_rows, up_full, preferred_element_type=jnp.float32)
        hidden = (jax.nn.silu(gate_value) * up_value).astype(jnp.bfloat16)
        hidden_blocks = hidden.reshape(row_count, GROUP, HID).astype(jnp.float32)
        slice_out = jnp.einsum('rgh,ghd->grd', hidden_blocks, down_slices.astype(jnp.float32))
        summed = jnp.sum(slice_out, axis=0)
        factor = jnp.where(filled, route_weight[safe_token, expert_index], jnp.zeros((), jnp.float32))
        scaled = summed * factor[:, None]
        return accumulated.at[safe_token].add(scaled), None

    accumulated, _ = lax.scan(one_expert, jnp.zeros((TOKENS, D), jnp.float32), expert_range)
    return accumulated.astype(jnp.bfloat16)
```

```python
import jax
import jax.numpy as jnp
from jax import lax
from jax.sharding import PartitionSpec as P

GROUPS = ((0,), (1, 2, 3))


def swap(value, axis, bits):
    size = lax.axis_size(axis)
    return lax.ppermute(value, axis, [(i, i ^ bits) for i in range(size)])


def route_shares(affinity):
    affinity_sum = jnp.sum(affinity, axis=1, keepdims=True)
    return (2.5 * affinity / affinity_sum).astype(jnp.bfloat16).astype(jnp.float32)


def dense_on_device(tokens, expert_ids, affinity, w_gate, w_up, w_down):
    node_count = lax.axis_size("node")
    local_count = lax.axis_size("local")
    group_size = local_count // 2
    expert_count = 2 * node_count
    tok_count, _ = expert_ids.shape
    rows = tok_count // local_count
    my_node = lax.axis_index("node")
    my_local = lax.axis_index("local")
    share = route_shares(affinity)
    expert_range = jnp.arange(expert_count, dtype=jnp.int32)
    hit = expert_ids[:, :, None] == expert_range[None, None, :]
    weight = jnp.sum(jnp.where(hit, share[:, :, None], 0.0), axis=1).astype(jnp.bfloat16)
    all_weight = lax.all_gather(weight, "node")
    mine = (expert_range == 2 * my_node + my_local // group_size).astype(jnp.float32)
    own_weight = jnp.sum(all_weight.astype(jnp.float32) * mine, axis=-1)
    own_weight = own_weight.reshape(node_count, local_count, rows)

    def quarter(index):
        return lax.dynamic_slice_in_dim(tokens, index * rows, rows, 0)

    own = [quarter(my_local ^ j) for j in range(local_count)]
    arrived = {k: swap(own[0], "node", k) for k in range(1, node_count)}
    results = {}
    for group in GROUPS:
        if group == (0,):
            parts = [own]
        else:
            joined = jnp.concatenate([arrived[k] for k in group], axis=0)
            others = [swap(joined, "local", j) for j in range(1, local_count)]
            parts = [[joined] + others]
        blocks = parts[0]
        x = jnp.concatenate(blocks, axis=0)
        gate = jnp.dot(x, w_gate[0], preferred_element_type=jnp.float32)
        up = jnp.dot(x, w_up[0], preferred_element_type=jnp.float32)
        both = jnp.concatenate([gate, up], axis=1)
        both = both + swap(both.astype(jnp.bfloat16), "cuts", 1).astype(jnp.float32)
        gate, up = both[:, : gate.shape[1]], both[:, gate.shape[1] :]
        hidden = (jax.nn.silu(gate) * up).astype(jnp.bfloat16)
        out = jnp.dot(hidden, w_down[0], preferred_element_type=jnp.float32)
        scale = jnp.concatenate(
            [own_weight[my_node ^ k, my_local ^ j] for j in range(local_count) for k in group]
        )
        out = (out * scale[:, None]).astype(jnp.bfloat16)
        step = len(group) * rows
        total = out[:step].astype(jnp.float32)
        for j in range(1, local_count):
            total = total + swap(out[j * step : (j + 1) * step], "local", j).astype(jnp.float32)
        for i, k in enumerate(group):
            results[k] = total[i * rows : (i + 1) * rows]
    final = results[0]
    for k in range(1, node_count):
        final = final + swap(results[k].astype(jnp.bfloat16), "node", k).astype(jnp.float32)
    return final.astype(jnp.bfloat16)


def slots_on_device(tokens, expert_ids, affinity, w_gate, w_up, w_down):
    node_count = lax.axis_size("node")
    local_count = lax.axis_size("local")
    group_size = local_count // 2
    expert_count = 2 * node_count
    tok_count, top_count = expert_ids.shape
    capacity = (5 * tok_count * top_count + 4 * expert_count - 1) // (4 * expert_count)
    half_width = tokens.shape[1]
    my_local = lax.axis_index("local")
    pair_index = my_local // group_size
    node_range = jnp.arange(node_count, dtype=jnp.int32)
    chosen_node = jnp.any(
        (expert_ids // 2)[:, :, None] == node_range[None, None, :], axis=1
    ).astype(jnp.float32)
    tok_range = jnp.arange(tok_count, dtype=jnp.int32)
    earlier = (tok_range[None, :] < tok_range[:, None]).astype(jnp.float32)
    node_rank = jnp.dot(earlier, chosen_node, precision=lax.Precision.HIGHEST)
    slot_range = jnp.arange(capacity, dtype=jnp.float32)
    dispatch = chosen_node[:, :, None] * (
        node_rank[:, :, None] == slot_range[None, None, :]
    ).astype(jnp.float32)
    outgoing = jnp.einsum(
        "tmc,td->mcd", dispatch.astype(jnp.bfloat16), tokens, preferred_element_type=jnp.float32
    ).astype(jnp.bfloat16)
    route_share = route_shares(affinity)
    pair_range = jnp.arange(2, dtype=jnp.int32)
    expert_grid = 2 * node_range[:, None] + pair_range[None, :]
    own_route = expert_ids[:, :, None, None] == expert_grid[None, None, :, :]
    pair_weight = jnp.sum(jnp.where(own_route, route_share[:, :, None, None], 0.0), axis=1)
    slot_weight = jnp.einsum(
        "tmc,tmp->mcp", dispatch, pair_weight, precision=lax.Precision.HIGHEST
    ).astype(jnp.bfloat16)
    arrived, arrived_weight = (
        lax.all_to_all(outgoing, "node", split_axis=0, concat_axis=0, tiled=True),
        lax.all_to_all(slot_weight, "node", split_axis=0, concat_axis=0, tiled=True),
    )
    expert_rows = arrived.reshape(node_count * capacity, half_width)
    gate_part = jnp.dot(expert_rows, w_gate[0], preferred_element_type=jnp.float32)
    up_part = jnp.dot(expert_rows, w_up[0], preferred_element_type=jnp.float32)
    gate_full, up_full = lax.psum((gate_part, up_part), "cuts")
    hidden = (jax.nn.silu(gate_full) * up_full).astype(jnp.bfloat16)
    slice_out = jnp.dot(hidden, w_down[0], preferred_element_type=jnp.float32)
    pick = (pair_range == pair_index).astype(jnp.float32)
    slot_scale = jnp.sum(arrived_weight.astype(jnp.float32) * pick[None, None, :], axis=2).reshape(
        node_count * capacity
    )
    weighted = (slice_out * slot_scale[:, None]).reshape(node_count, capacity, half_width)
    grouped = lax.psum_scatter(weighted, "local", scatter_dimension=2, tiled=True)
    returned = lax.all_to_all(grouped, "node", split_axis=0, concat_axis=0, tiled=True)
    partial_value = jnp.einsum("tmc,mcd->td", dispatch, returned, precision=lax.Precision.HIGHEST)
    summed = lax.all_to_all(partial_value, "local", split_axis=0, concat_axis=1, tiled=True)
    return summed.astype(jnp.bfloat16)


def on_device(tokens, expert_ids, affinity, w_gate, w_up, w_down):
    node_count = lax.axis_size("node")
    local_count = lax.axis_size("local")
    tok_count, top_count = expert_ids.shape
    expert_count = 2 * node_count
    capacity = (5 * tok_count * top_count + 4 * expert_count - 1) // (4 * expert_count)
    powers = all(size & (size - 1) == 0 for size in (node_count, local_count))
    everywhere = node_count == top_count // 2 and capacity >= tok_count
    chosen = dense_on_device if everywhere and powers and tok_count % local_count == 0 else slots_on_device
    return chosen(tokens, expert_ids, affinity, w_gate, w_up, w_down)


def solution(mesh):
    return jax.shard_map(
        on_device,
        mesh=mesh,
        in_specs=(
            P("node", "cuts"),
            P("node", None),
            P("node", None),
            P(("node", "local"), "cuts", None),
            P(("node", "local"), "cuts", None),
            P(("node", "local"), None, "cuts"),
        ),
        out_specs=P(("node", "local"), "cuts"),
        check_vma=False,
    )
```

```python
import jax
import jax.numpy as jnp
from jax import lax
from jax.experimental import pallas as pl
from jax.experimental.pallas import tpu as pltpu
from jax.sharding import PartitionSpec as P

LANES = 128


def swap(value, axis, bits):
    size = lax.axis_size(axis)
    return lax.ppermute(value, axis, [(i, i ^ bits) for i in range(size)])


def route_shares(affinity):
    affinity_sum = jnp.sum(affinity, axis=1, keepdims=True)
    return (2.5 * affinity / affinity_sum).astype(jnp.bfloat16).astype(jnp.float32)


def in_vmem(body, out_shapes, cost, *args):
    return pl.pallas_call(
        body,
        out_shape=out_shapes,
        in_specs=[pl.BlockSpec(memory_space=pltpu.VMEM)] * len(args),
        out_specs=jax.tree.map(lambda _: pl.BlockSpec(memory_space=pltpu.VMEM), out_shapes),
        compiler_params=pltpu.CompilerParams(vmem_limit_bytes=24 * 2**20),
        cost_estimate=pl.CostEstimate(flops=cost, bytes_accessed=2**20, transcendentals=0),
    )(*args)


def shape(*dims):
    return jax.ShapeDtypeStruct(dims, jnp.bfloat16)


def prepare(tokens, expert_ids, affinity, rows):
    tok_count, width = tokens.shape
    choices = expert_ids.shape[1]

    def body(tokens_hbm, ids_hbm, affinity_hbm, all_ref, share_ref, ids_ref, affinity_ref, sems):
        copies = [
            pltpu.make_async_copy(tokens_hbm, all_ref.at[:, :width], sems.at[0]),
            pltpu.make_async_copy(ids_hbm, ids_ref, sems.at[1]),
            pltpu.make_async_copy(affinity_hbm, affinity_ref, sems.at[2]),
        ]
        for copy in copies:
            copy.start()
        copies[1].wait()
        copies[2].wait()
        total = jnp.sum(affinity_ref[...], axis=0, keepdims=True)
        share = (2.5 * affinity_ref[...] / total).astype(jnp.bfloat16).astype(jnp.float32)
        ids = ids_ref[...]
        lane = lax.broadcasted_iota(jnp.int32, (LANES, tok_count), 0)
        weight = jnp.zeros((LANES, tok_count), jnp.float32)
        for c in range(choices):
            weight += jnp.where(ids[c : c + 1, :] == lane, share[c : c + 1, :], 0.0)
        all_ref[:, width:] = weight.T.astype(jnp.bfloat16)
        copies[0].wait()
        for i in range(tok_count // rows):

            @pl.when(lax.axis_index("local") == i)
            def _():
                share_ref[...] = all_ref[i * rows : (i + 1) * rows, :]

    return pl.pallas_call(
        body,
        out_shape=(shape(tok_count, width + LANES), shape(rows, width + LANES)),
        in_specs=[pl.BlockSpec(memory_space=pltpu.HBM)] * 3,
        out_specs=[pl.BlockSpec(memory_space=pltpu.VMEM)] * 2,
        scratch_shapes=[
            pltpu.VMEM((choices, tok_count), jnp.int32),
            pltpu.VMEM((choices, tok_count), jnp.float32),
            pltpu.SemaphoreType.DMA((3,)),
        ],
        compiler_params=pltpu.CompilerParams(vmem_limit_bytes=24 * 2**20),
        cost_estimate=pl.CostEstimate(flops=10**6, bytes_accessed=2**20, transcendentals=0),
    )(tokens, expert_ids.T, affinity.T)


def project(x, w_gate, w_up):
    count = x.shape[0]
    width, hid = w_gate.shape

    def body(x_ref, gate_ref, up_ref, out_ref):
        rows = x_ref[:, :width]
        for i, ref in enumerate((gate_ref, up_ref)):
            part = jnp.dot(rows, ref[...], preferred_element_type=jnp.float32)
            out_ref[:, i * hid : (i + 1) * hid] = part.astype(jnp.bfloat16)

    return in_vmem(body, shape(count, 2 * hid), 4 * count * width * hid, x, w_gate, w_up)


def finish(x, part, other, w_down, group_size):
    count = x.shape[0]
    hid, width = w_down.shape

    def body(x_ref, part_ref, other_ref, down_ref, out_ref):
        both = part_ref[...].astype(jnp.float32) + other_ref[...].astype(jnp.float32)
        gate, up = both[:, :hid], both[:, hid:]
        hidden = (gate / (1.0 + jnp.exp(-gate)) * up).astype(jnp.bfloat16)
        expert = 2 * lax.axis_index("node") + lax.axis_index("local") // group_size
        lane = lax.broadcasted_iota(jnp.int32, (count, LANES), 1)
        table = x_ref[:, width:].astype(jnp.float32)
        scale = jnp.sum(jnp.where(lane == expert, table, 0.0), axis=1, keepdims=True)
        out = jnp.dot(hidden, down_ref[...], preferred_element_type=jnp.float32)
        out_ref[...] = (out * scale).astype(jnp.bfloat16)

    return in_vmem(body, shape(count, width), 2 * count * width * hid, x, part, other, w_down)


def after(value, *others):
    return lax.optimization_barrier((value, *others))[0]


def dense_on_device(tokens, expert_ids, affinity, w_gate, w_up, w_down):
    node_count = lax.axis_size("node")
    local_count = lax.axis_size("local")
    group_size = local_count // 2
    tok_count, _ = expert_ids.shape
    rows = tok_count // local_count
    my_local = lax.axis_index("local")
    far = list(range(node_count - 1, 1, -1))

    def quarter(value, j):
        return lax.dynamic_slice_in_dim(value, (my_local ^ j) * rows, rows, 0)

    def experts(x):
        part = project(x, w_gate[0], w_up[0])
        return finish(x, part, swap(part, "cuts", 1), w_down[0], group_size)

    def gathered(value):
        others = [swap(value, "local", j) for j in range(1, local_count)]
        return jnp.concatenate([value] + others, axis=0)

    def reduced(blocks):
        total = blocks[0].astype(jnp.float32)
        for j in range(1, local_count):
            total = total + swap(blocks[j], "local", j).astype(jnp.float32)
        return total

    def split(value):
        step = value.shape[0] // local_count
        return [value[j * step : (j + 1) * step] for j in range(local_count)]

    everything, own = prepare(tokens, expert_ids, affinity, rows)
    arrived = dict(zip(far, lax.optimization_barrier([swap(own, "node", k) for k in far])))
    near = swap(everything, "node", 1)
    out_own = experts(everything)
    x = gathered(jnp.concatenate([arrived[k] for k in far], axis=0))
    out_near = experts(near)
    x = after(x, out_own, out_near)
    out_far = experts(x)
    near_back = swap(out_near, "node", 1)
    part = reduced(split(out_far)).astype(jnp.bfloat16)
    back = {k: swap(part[i * rows : (i + 1) * rows], "node", k) for i, k in enumerate(far)}
    both = (out_own.astype(jnp.float32) + near_back.astype(jnp.float32)).astype(jnp.bfloat16)
    own_blocks = [quarter(both, j) for j in range(local_count)]
    later = [swap(own_blocks[j], "local", j) for j in range(1, local_count)]
    total = sum(back[k].astype(jnp.float32) for k in far)
    total, *later = lax.optimization_barrier((total, *later))
    for value in [own_blocks[0], *later]:
        total = total + value.astype(jnp.float32)
    return total.astype(jnp.bfloat16)


def slots_on_device(tokens, expert_ids, affinity, w_gate, w_up, w_down):
    node_count = lax.axis_size("node")
    local_count = lax.axis_size("local")
    group_size = local_count // 2
    expert_count = 2 * node_count
    tok_count, top_count = expert_ids.shape
    capacity = (5 * tok_count * top_count + 4 * expert_count - 1) // (4 * expert_count)
    half_width = tokens.shape[1]
    my_local = lax.axis_index("local")
    pair_index = my_local // group_size
    node_range = jnp.arange(node_count, dtype=jnp.int32)
    chosen_node = jnp.any(
        (expert_ids // 2)[:, :, None] == node_range[None, None, :], axis=1
    ).astype(jnp.float32)
    tok_range = jnp.arange(tok_count, dtype=jnp.int32)
    earlier = (tok_range[None, :] < tok_range[:, None]).astype(jnp.float32)
    node_rank = jnp.dot(earlier, chosen_node, precision=lax.Precision.HIGHEST)
    slot_range = jnp.arange(capacity, dtype=jnp.float32)
    dispatch = chosen_node[:, :, None] * (
        node_rank[:, :, None] == slot_range[None, None, :]
    ).astype(jnp.float32)
    outgoing = jnp.einsum(
        "tmc,td->mcd", dispatch.astype(jnp.bfloat16), tokens, preferred_element_type=jnp.float32
    ).astype(jnp.bfloat16)
    route_share = route_shares(affinity)
    pair_range = jnp.arange(2, dtype=jnp.int32)
    expert_grid = 2 * node_range[:, None] + pair_range[None, :]
    own_route = expert_ids[:, :, None, None] == expert_grid[None, None, :, :]
    pair_weight = jnp.sum(jnp.where(own_route, route_share[:, :, None, None], 0.0), axis=1)
    slot_weight = jnp.einsum(
        "tmc,tmp->mcp", dispatch, pair_weight, precision=lax.Precision.HIGHEST
    ).astype(jnp.bfloat16)
    arrived, arrived_weight = (
        lax.all_to_all(outgoing, "node", split_axis=0, concat_axis=0, tiled=True),
        lax.all_to_all(slot_weight, "node", split_axis=0, concat_axis=0, tiled=True),
    )
    expert_rows = arrived.reshape(node_count * capacity, half_width)
    gate_part = jnp.dot(expert_rows, w_gate[0], preferred_element_type=jnp.float32)
    up_part = jnp.dot(expert_rows, w_up[0], preferred_element_type=jnp.float32)
    gate_full, up_full = lax.psum((gate_part, up_part), "cuts")
    hidden = (jax.nn.silu(gate_full) * up_full).astype(jnp.bfloat16)
    slice_out = jnp.dot(hidden, w_down[0], preferred_element_type=jnp.float32)
    pick = (pair_range == pair_index).astype(jnp.float32)
    slot_scale = jnp.sum(arrived_weight.astype(jnp.float32) * pick[None, None, :], axis=2).reshape(
        node_count * capacity
    )
    weighted = (slice_out * slot_scale[:, None]).reshape(node_count, capacity, half_width)
    grouped = lax.psum_scatter(weighted, "local", scatter_dimension=2, tiled=True)
    returned = lax.all_to_all(grouped, "node", split_axis=0, concat_axis=0, tiled=True)
    partial_value = jnp.einsum("tmc,mcd->td", dispatch, returned, precision=lax.Precision.HIGHEST)
    summed = lax.all_to_all(partial_value, "local", split_axis=0, concat_axis=1, tiled=True)
    return summed.astype(jnp.bfloat16)


def on_device(tokens, expert_ids, affinity, w_gate, w_up, w_down):
    node_count = lax.axis_size("node")
    local_count = lax.axis_size("local")
    tok_count, top_count = expert_ids.shape
    expert_count = 2 * node_count
    capacity = (5 * tok_count * top_count + 4 * expert_count - 1) // (4 * expert_count)
    powers = all(size & (size - 1) == 0 for size in (node_count, local_count))
    everywhere = node_count == top_count // 2 and capacity >= tok_count and expert_count <= LANES
    chosen = dense_on_device if everywhere and powers and tok_count % local_count == 0 else slots_on_device
    return chosen(tokens, expert_ids, affinity, w_gate, w_up, w_down)


def solution(mesh):
    return jax.shard_map(
        on_device,
        mesh=mesh,
        in_specs=(
            P("node", "cuts"),
            P("node", None),
            P("node", None),
            P(("node", "local"), "cuts", None),
            P(("node", "local"), "cuts", None),
            P(("node", "local"), None, "cuts"),
        ),
        out_specs=P(("node", "local"), "cuts"),
        check_vma=False,
    )
```

```python
import jax
import jax.numpy as jnp
from jax import lax
from jax.experimental import pallas as pl
from jax.experimental.pallas import tpu as pltpu
from jax.sharding import PartitionSpec as P

LANES = 128


def swap(value, axis, bits):
    size = lax.axis_size(axis)
    return lax.ppermute(value, axis, [(i, i ^ bits) for i in range(size)])


def route_shares(affinity):
    affinity_sum = jnp.sum(affinity, axis=1, keepdims=True)
    return (2.5 * affinity / affinity_sum).astype(jnp.bfloat16).astype(jnp.float32)


def in_vmem(body, out_shapes, cost, *args):
    return pl.pallas_call(
        body,
        out_shape=out_shapes,
        in_specs=[pl.BlockSpec(memory_space=pltpu.VMEM)] * len(args),
        out_specs=jax.tree.map(lambda _: pl.BlockSpec(memory_space=pltpu.VMEM), out_shapes),
        compiler_params=pltpu.CompilerParams(vmem_limit_bytes=24 * 2**20),
        cost_estimate=pl.CostEstimate(flops=cost, bytes_accessed=2**20, transcendentals=0),
    )(*args)


def in_hbm(value):
    return pltpu.with_memory_space_constraint(value, pltpu.HBM)


def shape(*dims):
    return jax.ShapeDtypeStruct(dims, jnp.bfloat16)


def prepare(tokens, expert_ids, affinity, rows):
    tok_count, width = tokens.shape
    choices = expert_ids.shape[1]

    def body(tokens_hbm, ids_hbm, affinity_hbm, all_ref, share_ref, ids_ref, affinity_ref, sems):
        copies = [
            pltpu.make_async_copy(tokens_hbm, all_ref.at[:, :width], sems.at[0]),
            pltpu.make_async_copy(ids_hbm, ids_ref, sems.at[1]),
            pltpu.make_async_copy(affinity_hbm, affinity_ref, sems.at[2]),
        ]
        for copy in copies:
            copy.start()
        copies[1].wait()
        copies[2].wait()
        total = jnp.sum(affinity_ref[...], axis=0, keepdims=True)
        share = (2.5 * affinity_ref[...] / total).astype(jnp.bfloat16).astype(jnp.float32)
        ids = ids_ref[...]
        lane = lax.broadcasted_iota(jnp.int32, (LANES, tok_count), 0)
        weight = jnp.zeros((LANES, tok_count), jnp.float32)
        for c in range(choices):
            weight += jnp.where(ids[c : c + 1, :] == lane, share[c : c + 1, :], 0.0)
        all_ref[:, width:] = weight.T.astype(jnp.bfloat16)
        copies[0].wait()
        for i in range(tok_count // rows):

            @pl.when(lax.axis_index("local") == i)
            def _():
                share_ref[...] = all_ref[i * rows : (i + 1) * rows, :]

    return pl.pallas_call(
        body,
        out_shape=(shape(tok_count, width + LANES), shape(rows, width + LANES)),
        in_specs=[pl.BlockSpec(memory_space=pltpu.HBM)] * 3,
        out_specs=[pl.BlockSpec(memory_space=pltpu.VMEM)] * 2,
        scratch_shapes=[
            pltpu.VMEM((choices, tok_count), jnp.int32),
            pltpu.VMEM((choices, tok_count), jnp.float32),
            pltpu.SemaphoreType.DMA((3,)),
        ],
        compiler_params=pltpu.CompilerParams(vmem_limit_bytes=24 * 2**20),
        cost_estimate=pl.CostEstimate(flops=10**6, bytes_accessed=2**20, transcendentals=0),
    )(*(in_hbm(value) for value in (tokens, expert_ids.T, affinity.T)))


def project_into(out_ref, rows, weight_refs, copies=()):
    hid = weight_refs[0].shape[1]
    for i, ref in enumerate(weight_refs):
        if copies:
            copies[i].wait()
        part = jnp.dot(rows, ref[...], preferred_element_type=jnp.float32)
        out_ref[:, i * hid : (i + 1) * hid] = part.astype(jnp.bfloat16)


def project(x, w_gate, w_up):
    count = x.shape[0]
    width, hid = w_gate.shape

    def body(x_ref, gate_ref, up_ref, out_ref):
        project_into(out_ref, x_ref[:, :width], (gate_ref, up_ref))

    return in_vmem(body, shape(count, 2 * hid), 4 * count * width * hid, x, w_gate, w_up)


def load_and_project(x, *weights):
    count = x.shape[0]
    width, hid = weights[0].shape

    def body(x_ref, gate_hbm, up_hbm, down_hbm, out_ref, gate_ref, up_ref, down_ref, sems):
        pairs = ((gate_hbm, gate_ref), (up_hbm, up_ref), (down_hbm, down_ref))
        copies = [pltpu.make_async_copy(src, dst, sems.at[i]) for i, (src, dst) in enumerate(pairs)]
        for copy in copies:
            copy.start()
        project_into(out_ref, x_ref[:, :width], (gate_ref, up_ref), copies)
        copies[2].wait()

    return pl.pallas_call(
        body,
        out_shape=(shape(count, 2 * hid), *(shape(*w.shape) for w in weights)),
        in_specs=[pl.BlockSpec(memory_space=pltpu.VMEM)] + [pl.BlockSpec(memory_space=pltpu.HBM)] * 3,
        out_specs=[pl.BlockSpec(memory_space=pltpu.VMEM)] * 4,
        scratch_shapes=[pltpu.SemaphoreType.DMA((3,))],
        compiler_params=pltpu.CompilerParams(vmem_limit_bytes=24 * 2**20),
    )(x, *(in_hbm(w) for w in weights))


def finish(x, part, other, w_down, group_size):
    count = x.shape[0]
    hid, width = w_down.shape

    def body(x_ref, part_ref, other_ref, down_ref, out_ref):
        both = part_ref[...].astype(jnp.float32) + other_ref[...].astype(jnp.float32)
        gate, up = both[:, :hid], both[:, hid:]
        hidden = (gate / (1.0 + jnp.exp(-gate)) * up).astype(jnp.bfloat16)
        expert = 2 * lax.axis_index("node") + lax.axis_index("local") // group_size
        lane = lax.broadcasted_iota(jnp.int32, (count, LANES), 1)
        table = x_ref[:, width:].astype(jnp.float32)
        scale = jnp.sum(jnp.where(lane == expert, table, 0.0), axis=1, keepdims=True)
        out = jnp.dot(hidden, down_ref[...], preferred_element_type=jnp.float32)
        out_ref[...] = (out * scale).astype(jnp.bfloat16)

    return in_vmem(body, shape(count, width), 2 * count * width * hid, x, part, other, w_down)


def after(value, *others):
    return lax.optimization_barrier((value, *others))[0]


def dense_on_device(tokens, expert_ids, affinity, w_gate, w_up, w_down):
    node_count = lax.axis_size("node")
    local_count = lax.axis_size("local")
    group_size = local_count // 2
    tok_count, _ = expert_ids.shape
    rows = tok_count // local_count
    my_local = lax.axis_index("local")
    far = list(range(node_count - 1, 1, -1))

    def quarter(value, j):
        return lax.dynamic_slice_in_dim(value, (my_local ^ j) * rows, rows, 0)

    def split(value):
        step = value.shape[0] // local_count
        return [value[j * step : (j + 1) * step] for j in range(local_count)]

    everything, own = prepare(tokens, expert_ids, affinity, rows)
    arrived = {k: swap(own, "node", k) for k in far}
    near = swap(everything, "node", 1)
    part_own, gate, up, down = load_and_project(everything, w_gate[0], w_up[0], w_down[0])

    def begin(x):
        part = project(x, gate, up)
        return x, part, swap(part, "cuts", 1)

    def complete(state, *others):
        x, part, other = state
        return finish(x, part, after(other, *others), down, group_size)

    def moved(blocks):
        return [swap(block, "local", j) for j, block in enumerate(blocks) if j]

    def summed(values):
        return sum(value.astype(jnp.float32) for value in values)

    arrived[far[0]] = after(arrived[far[0]], part_own)
    joined = jnp.concatenate([arrived[k] for k in far], axis=0)
    others = moved([joined] * local_count)
    near_state = begin(near)
    others[0] = after(others[0], near_state[1])
    out_near = complete(near_state)
    others[1] = after(others[1], out_near)
    near_back = swap(out_near, "node", 1)
    out_own = complete((everything, part_own, swap(part_own, "cuts", 1)))
    others[2] = after(others[2], out_own)
    x = jnp.concatenate([joined, *others], axis=0)
    out_far = complete(begin(x))
    blocks = split(out_far)
    others = moved(blocks)
    done = summed([blocks[0], *others]).astype(jnp.bfloat16)
    back = [swap(done[i * rows : (i + 1) * rows], "node", k) for i, k in enumerate(far)]
    near_back = after(near_back, done)
    both = (out_own.astype(jnp.float32) + near_back.astype(jnp.float32)).astype(jnp.bfloat16)
    blocks = [quarter(both, j) for j in range(local_count)]
    later = moved(blocks)
    total, *later = lax.optimization_barrier((summed(back), *later))
    return (total + summed([blocks[0], *later])).astype(jnp.bfloat16)


def slots_on_device(tokens, expert_ids, affinity, w_gate, w_up, w_down):
    node_count = lax.axis_size("node")
    local_count = lax.axis_size("local")
    group_size = local_count // 2
    expert_count = 2 * node_count
    tok_count, top_count = expert_ids.shape
    capacity = (5 * tok_count * top_count + 4 * expert_count - 1) // (4 * expert_count)
    half_width = tokens.shape[1]
    my_local = lax.axis_index("local")
    pair_index = my_local // group_size
    node_range = jnp.arange(node_count, dtype=jnp.int32)
    chosen_node = jnp.any(
        (expert_ids // 2)[:, :, None] == node_range[None, None, :], axis=1
    ).astype(jnp.float32)
    tok_range = jnp.arange(tok_count, dtype=jnp.int32)
    earlier = (tok_range[None, :] < tok_range[:, None]).astype(jnp.float32)
    node_rank = jnp.dot(earlier, chosen_node, precision=lax.Precision.HIGHEST)
    slot_range = jnp.arange(capacity, dtype=jnp.float32)
    dispatch = chosen_node[:, :, None] * (
        node_rank[:, :, None] == slot_range[None, None, :]
    ).astype(jnp.float32)
    outgoing = jnp.einsum(
        "tmc,td->mcd", dispatch.astype(jnp.bfloat16), tokens, preferred_element_type=jnp.float32
    ).astype(jnp.bfloat16)
    route_share = route_shares(affinity)
    pair_range = jnp.arange(2, dtype=jnp.int32)
    expert_grid = 2 * node_range[:, None] + pair_range[None, :]
    own_route = expert_ids[:, :, None, None] == expert_grid[None, None, :, :]
    pair_weight = jnp.sum(jnp.where(own_route, route_share[:, :, None, None], 0.0), axis=1)
    slot_weight = jnp.einsum(
        "tmc,tmp->mcp", dispatch, pair_weight, precision=lax.Precision.HIGHEST
    ).astype(jnp.bfloat16)
    arrived, arrived_weight = (
        lax.all_to_all(outgoing, "node", split_axis=0, concat_axis=0, tiled=True),
        lax.all_to_all(slot_weight, "node", split_axis=0, concat_axis=0, tiled=True),
    )
    expert_rows = arrived.reshape(node_count * capacity, half_width)
    gate_part = jnp.dot(expert_rows, w_gate[0], preferred_element_type=jnp.float32)
    up_part = jnp.dot(expert_rows, w_up[0], preferred_element_type=jnp.float32)
    gate_full, up_full = lax.psum((gate_part, up_part), "cuts")
    hidden = (jax.nn.silu(gate_full) * up_full).astype(jnp.bfloat16)
    slice_out = jnp.dot(hidden, w_down[0], preferred_element_type=jnp.float32)
    pick = (pair_range == pair_index).astype(jnp.float32)
    slot_scale = jnp.sum(arrived_weight.astype(jnp.float32) * pick[None, None, :], axis=2).reshape(
        node_count * capacity
    )
    weighted = (slice_out * slot_scale[:, None]).reshape(node_count, capacity, half_width)
    grouped = lax.psum_scatter(weighted, "local", scatter_dimension=2, tiled=True)
    returned = lax.all_to_all(grouped, "node", split_axis=0, concat_axis=0, tiled=True)
    partial_value = jnp.einsum("tmc,mcd->td", dispatch, returned, precision=lax.Precision.HIGHEST)
    summed = lax.all_to_all(partial_value, "local", split_axis=0, concat_axis=1, tiled=True)
    return summed.astype(jnp.bfloat16)


def on_device(tokens, expert_ids, affinity, w_gate, w_up, w_down):
    node_count = lax.axis_size("node")
    local_count = lax.axis_size("local")
    tok_count, top_count = expert_ids.shape
    expert_count = 2 * node_count
    capacity = (5 * tok_count * top_count + 4 * expert_count - 1) // (4 * expert_count)
    powers = all(size & (size - 1) == 0 for size in (node_count, local_count))
    everywhere = node_count == top_count // 2 and capacity >= tok_count and expert_count <= LANES
    chosen = dense_on_device if everywhere and powers and tok_count % local_count == 0 else slots_on_device
    return chosen(tokens, expert_ids, affinity, w_gate, w_up, w_down)


def solution(mesh):
    return jax.shard_map(
        on_device,
        mesh=mesh,
        in_specs=(
            P("node", "cuts"),
            P("node", None),
            P("node", None),
            P(("node", "local"), "cuts", None),
            P(("node", "local"), "cuts", None),
            P(("node", "local"), None, "cuts"),
        ),
        out_specs=P(("node", "local"), "cuts"),
        check_vma=False,
    )
```

```python
import jax
import jax.numpy as jnp
from jax import lax
from jax.experimental import pallas as pl
from jax.experimental.pallas import tpu as pltpu
from jax.sharding import PartitionSpec as P

LANES = 128


def swap(value, axis, bits):
    size = lax.axis_size(axis)
    return lax.ppermute(value, axis, [(i, i ^ bits) for i in range(size)])


def route_shares(affinity):
    affinity_sum = jnp.sum(affinity, axis=1, keepdims=True)
    return (2.5 * affinity / affinity_sum).astype(jnp.bfloat16).astype(jnp.float32)


def in_vmem(body, out_shapes, cost, *args):
    return pl.pallas_call(
        body,
        out_shape=out_shapes,
        in_specs=[pl.BlockSpec(memory_space=pltpu.VMEM)] * len(args),
        out_specs=jax.tree.map(lambda _: pl.BlockSpec(memory_space=pltpu.VMEM), out_shapes),
        compiler_params=pltpu.CompilerParams(vmem_limit_bytes=24 * 2**20),
        cost_estimate=pl.CostEstimate(flops=cost, bytes_accessed=2**20, transcendentals=0),
    )(*args)


def in_hbm(value):
    return pltpu.with_memory_space_constraint(value, pltpu.HBM)


def shape(*dims):
    return jax.ShapeDtypeStruct(dims, jnp.bfloat16)


def prepare(tokens, expert_ids, affinity, rows):
    tok_count, width = tokens.shape
    choices = expert_ids.shape[1]

    parts = tok_count // rows

    def body(tokens_hbm, ids_hbm, affinity_hbm, all_ref, share_ref, opposite_ref, ids_ref, affinity_ref, sems):
        copies = [
            pltpu.make_async_copy(tokens_hbm, all_ref.at[:, :width], sems.at[0]),
            pltpu.make_async_copy(ids_hbm, ids_ref, sems.at[1]),
            pltpu.make_async_copy(affinity_hbm, affinity_ref, sems.at[2]),
        ]
        for copy in copies:
            copy.start()
        copies[1].wait()
        copies[2].wait()
        total = jnp.sum(affinity_ref[...], axis=0, keepdims=True)
        share = (2.5 * affinity_ref[...] / total).astype(jnp.bfloat16).astype(jnp.float32)
        ids = ids_ref[...]
        lane = lax.broadcasted_iota(jnp.int32, (LANES, tok_count), 0)
        weight = jnp.zeros((LANES, tok_count), jnp.float32)
        for c in range(choices):
            weight += jnp.where(ids[c : c + 1, :] == lane, share[c : c + 1, :], 0.0)
        all_ref[:, width:] = weight.T.astype(jnp.bfloat16)
        copies[0].wait()
        for i in range(parts):
            other = i ^ (parts - 1)

            @pl.when(lax.axis_index("local") == i)
            def _():
                share_ref[...] = all_ref[i * rows : (i + 1) * rows, :]
                opposite_ref[...] = all_ref[other * rows : (other + 1) * rows, :]

    return pl.pallas_call(
        body,
        out_shape=(shape(tok_count, width + LANES), *[shape(rows, width + LANES)] * 2),
        in_specs=[pl.BlockSpec(memory_space=pltpu.HBM)] * 3,
        out_specs=[pl.BlockSpec(memory_space=pltpu.VMEM)] * 3,
        scratch_shapes=[
            pltpu.VMEM((choices, tok_count), jnp.int32),
            pltpu.VMEM((choices, tok_count), jnp.float32),
            pltpu.SemaphoreType.DMA((3,)),
        ],
        compiler_params=pltpu.CompilerParams(vmem_limit_bytes=24 * 2**20),
        cost_estimate=pl.CostEstimate(flops=10**6, bytes_accessed=2**20, transcendentals=0),
    )(*(in_hbm(value) for value in (tokens, expert_ids.T, affinity.T)))


def project_into(out_ref, rows, weight_refs, copies=()):
    hid = weight_refs[0].shape[1]
    for i, ref in enumerate(weight_refs):
        if copies:
            copies[i].wait()
        part = jnp.dot(rows, ref[...], preferred_element_type=jnp.float32)
        out_ref[:, i * hid : (i + 1) * hid] = part.astype(jnp.bfloat16)


def project(x, w_gate, w_up):
    count = x.shape[0]
    width, hid = w_gate.shape

    def body(x_ref, gate_ref, up_ref, out_ref):
        project_into(out_ref, x_ref[:, :width], (gate_ref, up_ref))

    return in_vmem(body, shape(count, 2 * hid), 4 * count * width * hid, x, w_gate, w_up)


def load_and_project(x, *weights):
    count = x.shape[0]
    width, hid = weights[0].shape

    def body(x_ref, gate_hbm, up_hbm, down_hbm, out_ref, gate_ref, up_ref, down_ref, sems):
        pairs = ((gate_hbm, gate_ref), (up_hbm, up_ref), (down_hbm, down_ref))
        copies = [pltpu.make_async_copy(src, dst, sems.at[i]) for i, (src, dst) in enumerate(pairs)]
        for copy in copies:
            copy.start()
        project_into(out_ref, x_ref[:, :width], (gate_ref, up_ref), copies)
        copies[2].wait()

    return pl.pallas_call(
        body,
        out_shape=(shape(count, 2 * hid), *(shape(*w.shape) for w in weights)),
        in_specs=[pl.BlockSpec(memory_space=pltpu.VMEM)] + [pl.BlockSpec(memory_space=pltpu.HBM)] * 3,
        out_specs=[pl.BlockSpec(memory_space=pltpu.VMEM)] * 4,
        scratch_shapes=[pltpu.SemaphoreType.DMA((3,))],
        compiler_params=pltpu.CompilerParams(vmem_limit_bytes=24 * 2**20),
    )(x, *(in_hbm(w) for w in weights))


def finish(x, part, other, w_down, group_size):
    count = x.shape[0]
    hid, width = w_down.shape

    def body(x_ref, part_ref, other_ref, down_ref, out_ref):
        both = part_ref[...].astype(jnp.float32) + other_ref[...].astype(jnp.float32)
        gate, up = both[:, :hid], both[:, hid:]
        hidden = (gate / (1.0 + jnp.exp(-gate)) * up).astype(jnp.bfloat16)
        expert = 2 * lax.axis_index("node") + lax.axis_index("local") // group_size
        lane = lax.broadcasted_iota(jnp.int32, (count, LANES), 1)
        table = x_ref[:, width:].astype(jnp.float32)
        scale = jnp.sum(jnp.where(lane == expert, table, 0.0), axis=1, keepdims=True)
        out = jnp.dot(hidden, down_ref[...], preferred_element_type=jnp.float32)
        out_ref[...] = (out * scale).astype(jnp.bfloat16)

    return in_vmem(body, shape(count, width), 2 * count * width * hid, x, part, other, w_down)


def merge(rows, partners, *values):
    count, width = values[0].shape
    parts = count // rows

    def body(own_ref, near_ref, direct_ref, *out_refs):
        for i in range(parts):

            @pl.when(lax.axis_index("local") == i)
            def _():
                for j, ref in zip((0, *partners), out_refs):
                    where = pl.ds((i ^ j) * rows, rows)
                    total = own_ref[where, :].astype(jnp.float32) + near_ref[where, :].astype(jnp.float32)
                    if j == parts - 1:
                        total += direct_ref[...].astype(jnp.float32)
                    ref[...] = total.astype(jnp.bfloat16)

    return in_vmem(body, tuple(shape(rows, width) for _ in range(parts)), 3 * count * width, *values)


def after(value, *others):
    return lax.optimization_barrier((value, *others))[0]


def dense_on_device(tokens, expert_ids, affinity, w_gate, w_up, w_down):
    node_count = lax.axis_size("node")
    local_count = lax.axis_size("local")
    group_size = local_count // 2
    tok_count, _ = expert_ids.shape
    rows = tok_count // local_count
    far = list(range(node_count - 1, 1, -1))

    def split(value):
        step = value.shape[0] // local_count
        return [value[j * step : (j + 1) * step] for j in range(local_count)]

    everything, own, opposite = prepare(tokens, expert_ids, affinity, rows)
    arrived = {k: swap(own, "node", k) for k in far}
    direct = swap(opposite, "node", far[-1])
    near = swap(everything, "node", 1)
    part_own, gate, up, down = load_and_project(everything, w_gate[0], w_up[0], w_down[0])

    def begin(x):
        part = project(x, gate, up)
        return x, part, swap(part, "cuts", 1)

    def complete(state, *others):
        x, part, other = state
        return finish(x, part, after(other, *others), down, group_size)

    partners = sorted(range(1, local_count), key=lambda j: (-j.bit_count(), j))

    def exchanged(blocks):
        return [swap(block, "local", j) for j, block in zip(partners, blocks)]

    def moved(blocks):
        return exchanged([blocks[j] for j in partners])

    def summed(values):
        return sum(value.astype(jnp.float32) for value in values)

    arrived[far[0]] = after(arrived[far[0]], part_own)
    joined = jnp.concatenate([arrived[k] for k in far], axis=0)
    others = moved([joined] * (local_count - 1) + [jnp.concatenate([arrived[k] for k in far[:-1]], axis=0)])
    out_own = complete((everything, part_own, swap(part_own, "cuts", 1)))
    x_near, part_near, other_near = begin(near)
    *others, direct, part_near, out_own = lax.optimization_barrier((*others, direct, part_near, out_own))
    by_partner = [joined] + [others[partners.index(j)] for j in range(1, local_count)] + [direct]
    state = begin(jnp.concatenate(by_partner, axis=0))
    out_far = complete(state)
    out_near = complete((x_near, part_near, other_near), out_far)
    near_back = swap(out_near, "node", 1)
    blocks = split(out_far)
    direct_back = swap(blocks[-1][-rows:], "node", far[-1])
    blocks[-1] = blocks[-1][:-rows]
    first, *others = moved(blocks)
    begun = summed([blocks[0][:-rows], first])
    begun, *others = lax.optimization_barrier((begun, *others))
    done = [begun[i * rows : (i + 1) * rows] for i in range(len(far) - 1)] + [blocks[0][-rows:].astype(jnp.float32)]
    done = [(v + summed([o[i * rows : (i + 1) * rows] for o in others])).astype(jnp.bfloat16) for i, v in enumerate(done)]
    back = [swap(value, "node", k) for value, k in zip(done, far)]
    out_own = after(out_own, *done)
    mine, *blocks = merge(rows, partners, out_own, near_back, direct_back)
    later = exchanged(blocks)
    total, *later = lax.optimization_barrier((summed(back), *later))
    return (total + summed([mine, *later])).astype(jnp.bfloat16)


def slots_on_device(tokens, expert_ids, affinity, w_gate, w_up, w_down):
    node_count = lax.axis_size("node")
    local_count = lax.axis_size("local")
    group_size = local_count // 2
    expert_count = 2 * node_count
    tok_count, top_count = expert_ids.shape
    capacity = (5 * tok_count * top_count + 4 * expert_count - 1) // (4 * expert_count)
    half_width = tokens.shape[1]
    my_local = lax.axis_index("local")
    pair_index = my_local // group_size
    node_range = jnp.arange(node_count, dtype=jnp.int32)
    chosen_node = jnp.any(
        (expert_ids // 2)[:, :, None] == node_range[None, None, :], axis=1
    ).astype(jnp.float32)
    tok_range = jnp.arange(tok_count, dtype=jnp.int32)
    earlier = (tok_range[None, :] < tok_range[:, None]).astype(jnp.float32)
    node_rank = jnp.dot(earlier, chosen_node, precision=lax.Precision.HIGHEST)
    slot_range = jnp.arange(capacity, dtype=jnp.float32)
    dispatch = chosen_node[:, :, None] * (
        node_rank[:, :, None] == slot_range[None, None, :]
    ).astype(jnp.float32)
    outgoing = jnp.einsum(
        "tmc,td->mcd", dispatch.astype(jnp.bfloat16), tokens, preferred_element_type=jnp.float32
    ).astype(jnp.bfloat16)
    route_share = route_shares(affinity)
    pair_range = jnp.arange(2, dtype=jnp.int32)
    expert_grid = 2 * node_range[:, None] + pair_range[None, :]
    own_route = expert_ids[:, :, None, None] == expert_grid[None, None, :, :]
    pair_weight = jnp.sum(jnp.where(own_route, route_share[:, :, None, None], 0.0), axis=1)
    slot_weight = jnp.einsum(
        "tmc,tmp->mcp", dispatch, pair_weight, precision=lax.Precision.HIGHEST
    ).astype(jnp.bfloat16)
    arrived, arrived_weight = (
        lax.all_to_all(outgoing, "node", split_axis=0, concat_axis=0, tiled=True),
        lax.all_to_all(slot_weight, "node", split_axis=0, concat_axis=0, tiled=True),
    )
    expert_rows = arrived.reshape(node_count * capacity, half_width)
    gate_part = jnp.dot(expert_rows, w_gate[0], preferred_element_type=jnp.float32)
    up_part = jnp.dot(expert_rows, w_up[0], preferred_element_type=jnp.float32)
    gate_full, up_full = lax.psum((gate_part, up_part), "cuts")
    hidden = (jax.nn.silu(gate_full) * up_full).astype(jnp.bfloat16)
    slice_out = jnp.dot(hidden, w_down[0], preferred_element_type=jnp.float32)
    pick = (pair_range == pair_index).astype(jnp.float32)
    slot_scale = jnp.sum(arrived_weight.astype(jnp.float32) * pick[None, None, :], axis=2).reshape(
        node_count * capacity
    )
    weighted = (slice_out * slot_scale[:, None]).reshape(node_count, capacity, half_width)
    grouped = lax.psum_scatter(weighted, "local", scatter_dimension=2, tiled=True)
    returned = lax.all_to_all(grouped, "node", split_axis=0, concat_axis=0, tiled=True)
    partial_value = jnp.einsum("tmc,mcd->td", dispatch, returned, precision=lax.Precision.HIGHEST)
    summed = lax.all_to_all(partial_value, "local", split_axis=0, concat_axis=1, tiled=True)
    return summed.astype(jnp.bfloat16)


def on_device(tokens, expert_ids, affinity, w_gate, w_up, w_down):
    node_count = lax.axis_size("node")
    local_count = lax.axis_size("local")
    tok_count, top_count = expert_ids.shape
    expert_count = 2 * node_count
    capacity = (5 * tok_count * top_count + 4 * expert_count - 1) // (4 * expert_count)
    powers = all(size & (size - 1) == 0 for size in (node_count, local_count))
    everywhere = node_count == top_count // 2 and capacity >= tok_count and expert_count <= LANES
    chosen = dense_on_device if everywhere and powers and tok_count % local_count == 0 else slots_on_device
    return chosen(tokens, expert_ids, affinity, w_gate, w_up, w_down)


def solution(mesh):
    return jax.shard_map(
        on_device,
        mesh=mesh,
        in_specs=(
            P("node", "cuts"),
            P("node", None),
            P("node", None),
            P(("node", "local"), "cuts", None),
            P(("node", "local"), "cuts", None),
            P(("node", "local"), None, "cuts"),
        ),
        out_specs=P(("node", "local"), "cuts"),
        check_vma=False,
    )
```

```python
import jax
import jax.numpy as jnp
from jax import lax
from jax.experimental import pallas as pl
from jax.experimental.pallas import tpu as pltpu
from jax.sharding import PartitionSpec as P

LANES = 128


def swap(value, axis, bits):
    size = lax.axis_size(axis)
    return lax.ppermute(value, axis, [(i, i ^ bits) for i in range(size)])


def route_shares(affinity):
    affinity_sum = jnp.sum(affinity, axis=1, keepdims=True)
    return (2.5 * affinity / affinity_sum).astype(jnp.bfloat16).astype(jnp.float32)


def in_vmem(body, out_shapes, cost, *args):
    return pl.pallas_call(
        body,
        out_shape=out_shapes,
        in_specs=[pl.BlockSpec(memory_space=pltpu.VMEM)] * len(args),
        out_specs=jax.tree.map(lambda _: pl.BlockSpec(memory_space=pltpu.VMEM), out_shapes),
        compiler_params=pltpu.CompilerParams(vmem_limit_bytes=24 * 2**20),
        cost_estimate=pl.CostEstimate(flops=cost, bytes_accessed=2**20, transcendentals=0),
    )(*args)


def in_hbm(value):
    return pltpu.with_memory_space_constraint(value, pltpu.HBM)


def shape(*dims):
    return jax.ShapeDtypeStruct(dims, jnp.bfloat16)


def prepare(tokens, expert_ids, affinity, rows):
    tok_count, width = tokens.shape
    choices = expert_ids.shape[1]

    parts = tok_count // rows

    def body(tokens_hbm, ids_hbm, affinity_hbm, all_ref, share_ref, opposite_ref, ids_ref, affinity_ref, sems):
        copies = [
            pltpu.make_async_copy(tokens_hbm, all_ref.at[:, :width], sems.at[0]),
            pltpu.make_async_copy(ids_hbm, ids_ref, sems.at[1]),
            pltpu.make_async_copy(affinity_hbm, affinity_ref, sems.at[2]),
        ]
        for copy in copies:
            copy.start()
        copies[1].wait()
        copies[2].wait()
        total = jnp.sum(affinity_ref[...], axis=0, keepdims=True)
        share = (2.5 * affinity_ref[...] / total).astype(jnp.bfloat16).astype(jnp.float32)
        ids = ids_ref[...]
        lane = lax.broadcasted_iota(jnp.int32, (LANES, tok_count), 0)
        weight = jnp.zeros((LANES, tok_count), jnp.float32)
        for c in range(choices):
            weight += jnp.where(ids[c : c + 1, :] == lane, share[c : c + 1, :], 0.0)
        all_ref[:, width:] = weight.T.astype(jnp.bfloat16)
        copies[0].wait()
        for i in range(parts):
            other = i ^ (parts - 1)

            @pl.when(lax.axis_index("local") == i)
            def _():
                share_ref[...] = all_ref[i * rows : (i + 1) * rows, :]
                opposite_ref[...] = all_ref[other * rows : (other + 1) * rows, :]

    return pl.pallas_call(
        body,
        out_shape=(shape(tok_count, width + LANES), *[shape(rows, width + LANES)] * 2),
        in_specs=[pl.BlockSpec(memory_space=pltpu.HBM)] * 3,
        out_specs=[pl.BlockSpec(memory_space=pltpu.VMEM)] * 3,
        scratch_shapes=[
            pltpu.VMEM((choices, tok_count), jnp.int32),
            pltpu.VMEM((choices, tok_count), jnp.float32),
            pltpu.SemaphoreType.DMA((3,)),
        ],
        compiler_params=pltpu.CompilerParams(vmem_limit_bytes=24 * 2**20),
        cost_estimate=pl.CostEstimate(flops=10**6, bytes_accessed=2**20, transcendentals=0),
    )(*(in_hbm(value) for value in (tokens, expert_ids.T, affinity.T)))


def project_into(out_ref, rows, weight_refs, copies=()):
    hid = weight_refs[0].shape[1]
    for i, ref in enumerate(weight_refs):
        if copies:
            copies[i].wait()
        part = jnp.dot(rows, ref[...], preferred_element_type=jnp.float32)
        out_ref[:, i * hid : (i + 1) * hid] = part.astype(jnp.bfloat16)


def project(x, w_gate, w_up):
    count = x.shape[0]
    width, hid = w_gate.shape

    def body(x_ref, gate_ref, up_ref, out_ref):
        project_into(out_ref, x_ref[:, :width], (gate_ref, up_ref))

    return in_vmem(body, shape(count, 2 * hid), 4 * count * width * hid, x, w_gate, w_up)


def load_and_project(x, *weights):
    count = x.shape[0]
    width, hid = weights[0].shape

    def body(x_ref, gate_hbm, up_hbm, down_hbm, out_ref, gate_ref, up_ref, down_ref, sems):
        pairs = ((gate_hbm, gate_ref), (up_hbm, up_ref), (down_hbm, down_ref))
        copies = [pltpu.make_async_copy(src, dst, sems.at[i]) for i, (src, dst) in enumerate(pairs)]
        for copy in copies:
            copy.start()
        project_into(out_ref, x_ref[:, :width], (gate_ref, up_ref), copies)
        copies[2].wait()

    return pl.pallas_call(
        body,
        out_shape=(shape(count, 2 * hid), *(shape(*w.shape) for w in weights)),
        in_specs=[pl.BlockSpec(memory_space=pltpu.VMEM)] + [pl.BlockSpec(memory_space=pltpu.HBM)] * 3,
        out_specs=[pl.BlockSpec(memory_space=pltpu.VMEM)] * 4,
        scratch_shapes=[pltpu.SemaphoreType.DMA((3,))],
        compiler_params=pltpu.CompilerParams(vmem_limit_bytes=24 * 2**20),
    )(x, *(in_hbm(w) for w in weights))


def finish(x, part, other, w_down, group_size):
    count = x.shape[0]
    hid, width = w_down.shape

    def body(x_ref, part_ref, other_ref, down_ref, out_ref):
        both = part_ref[...].astype(jnp.float32) + other_ref[...].astype(jnp.float32)
        gate, up = both[:, :hid], both[:, hid:]
        hidden = (gate / (1.0 + jnp.exp(-gate)) * up).astype(jnp.bfloat16)
        expert = 2 * lax.axis_index("node") + lax.axis_index("local") // group_size
        lane = lax.broadcasted_iota(jnp.int32, (count, LANES), 1)
        table = x_ref[:, width:].astype(jnp.float32)
        scale = jnp.sum(jnp.where(lane == expert, table, 0.0), axis=1, keepdims=True)
        out = jnp.dot(hidden, down_ref[...], preferred_element_type=jnp.float32)
        out_ref[...] = (out * scale).astype(jnp.bfloat16)

    return in_vmem(body, shape(count, width), 2 * count * width * hid, x, part, other, w_down)


def merge(rows, partners, *values):
    count, width = values[0].shape
    parts = count // rows

    def body(own_ref, near_ref, direct_ref, *out_refs):
        for i in range(parts):

            @pl.when(lax.axis_index("local") == i)
            def _():
                for j, ref in zip((0, *partners), out_refs):
                    where = pl.ds((i ^ j) * rows, rows)
                    total = own_ref[where, :].astype(jnp.float32) + near_ref[where, :].astype(jnp.float32)
                    if j == parts - 1:
                        total += direct_ref[...].astype(jnp.float32)
                    ref[...] = total.astype(jnp.bfloat16)

    return in_vmem(body, tuple(shape(rows, width) for _ in range(parts)), 3 * count * width, *values)


def after(value, *others):
    return lax.optimization_barrier((value, *others))[0]


def dense_on_device(tokens, expert_ids, affinity, w_gate, w_up, w_down):
    node_count = lax.axis_size("node")
    local_count = lax.axis_size("local")
    group_size = local_count // 2
    tok_count, _ = expert_ids.shape
    rows = tok_count // local_count
    far = list(range(node_count - 1, 1, -1))

    def split(value):
        step = value.shape[0] // local_count
        return [value[j * step : (j + 1) * step] for j in range(local_count)]

    everything, own, opposite = prepare(tokens, expert_ids, affinity, rows)
    arrived = {k: swap(own, "node", k) for k in far}
    near = swap(everything, "node", 1)
    part_own, gate, up, down = load_and_project(everything, w_gate[0], w_up[0], w_down[0])

    def begin(x):
        part = project(x, gate, up)
        return x, part, swap(part, "cuts", 1)

    def complete(state, *others):
        x, part, other = state
        return finish(x, part, after(other, *others), down, group_size)

    partners = sorted(range(1, local_count), key=lambda j: (-j.bit_count(), j))

    def exchanged(blocks):
        return [swap(block, "local", j) for j, block in zip(partners, blocks)]

    def moved(blocks):
        return exchanged([blocks[j] for j in partners])

    def summed(values):
        return sum(value.astype(jnp.float32) for value in values)

    arrived[far[0]] = after(arrived[far[0]], part_own)
    joined = jnp.concatenate([arrived[k] for k in far], axis=0)
    others = moved([joined] * (local_count - 1) + [jnp.concatenate([arrived[k] for k in far[:-1]], axis=0)])
    out_own = complete((everything, part_own, swap(part_own, "cuts", 1)))
    direct = swap(after(opposite, out_own), "node", far[-1])
    near_state = begin(near)
    others[1] = after(others[1], near_state[1])
    others[2] = after(others[2], near_state[2])
    by_partner = [joined] + [others[partners.index(j)] for j in range(1, local_count)] + [direct]
    state = begin(after(jnp.concatenate(by_partner, axis=0), out_own))
    out_near = complete(near_state, state[1])
    near_back = swap(out_near, "node", 1)
    out_far = complete(state, out_near)
    blocks = split(out_far)
    direct_back = swap(blocks[-1][-rows:], "node", far[-1])
    blocks[-1] = blocks[-1][:-rows]
    first, *others = moved(blocks)
    begun = summed([blocks[0][:-rows], first])
    begun, *others = lax.optimization_barrier((begun, *others))
    done = [begun[i * rows : (i + 1) * rows] for i in range(len(far) - 1)] + [blocks[0][-rows:].astype(jnp.float32)]
    done = [(v + summed([o[i * rows : (i + 1) * rows] for o in others])).astype(jnp.bfloat16) for i, v in enumerate(done)]
    back = [swap(value, "node", k) for value, k in zip(done, far)]
    out_own = after(out_own, *done)
    mine, *blocks = merge(rows, partners, out_own, near_back, direct_back)
    later = exchanged(blocks)
    total, *later = lax.optimization_barrier((summed(back), *later))
    return (total + summed([mine, *later])).astype(jnp.bfloat16)


def slots_on_device(tokens, expert_ids, affinity, w_gate, w_up, w_down):
    node_count = lax.axis_size("node")
    local_count = lax.axis_size("local")
    group_size = local_count // 2
    expert_count = 2 * node_count
    tok_count, top_count = expert_ids.shape
    capacity = (5 * tok_count * top_count + 4 * expert_count - 1) // (4 * expert_count)
    half_width = tokens.shape[1]
    my_local = lax.axis_index("local")
    pair_index = my_local // group_size
    node_range = jnp.arange(node_count, dtype=jnp.int32)
    chosen_node = jnp.any(
        (expert_ids // 2)[:, :, None] == node_range[None, None, :], axis=1
    ).astype(jnp.float32)
    tok_range = jnp.arange(tok_count, dtype=jnp.int32)
    earlier = (tok_range[None, :] < tok_range[:, None]).astype(jnp.float32)
    node_rank = jnp.dot(earlier, chosen_node, precision=lax.Precision.HIGHEST)
    slot_range = jnp.arange(capacity, dtype=jnp.float32)
    dispatch = chosen_node[:, :, None] * (
        node_rank[:, :, None] == slot_range[None, None, :]
    ).astype(jnp.float32)
    outgoing = jnp.einsum(
        "tmc,td->mcd", dispatch.astype(jnp.bfloat16), tokens, preferred_element_type=jnp.float32
    ).astype(jnp.bfloat16)
    route_share = route_shares(affinity)
    pair_range = jnp.arange(2, dtype=jnp.int32)
    expert_grid = 2 * node_range[:, None] + pair_range[None, :]
    own_route = expert_ids[:, :, None, None] == expert_grid[None, None, :, :]
    pair_weight = jnp.sum(jnp.where(own_route, route_share[:, :, None, None], 0.0), axis=1)
    slot_weight = jnp.einsum(
        "tmc,tmp->mcp", dispatch, pair_weight, precision=lax.Precision.HIGHEST
    ).astype(jnp.bfloat16)
    arrived, arrived_weight = (
        lax.all_to_all(outgoing, "node", split_axis=0, concat_axis=0, tiled=True),
        lax.all_to_all(slot_weight, "node", split_axis=0, concat_axis=0, tiled=True),
    )
    expert_rows = arrived.reshape(node_count * capacity, half_width)
    gate_part = jnp.dot(expert_rows, w_gate[0], preferred_element_type=jnp.float32)
    up_part = jnp.dot(expert_rows, w_up[0], preferred_element_type=jnp.float32)
    gate_full, up_full = lax.psum((gate_part, up_part), "cuts")
    hidden = (jax.nn.silu(gate_full) * up_full).astype(jnp.bfloat16)
    slice_out = jnp.dot(hidden, w_down[0], preferred_element_type=jnp.float32)
    pick = (pair_range == pair_index).astype(jnp.float32)
    slot_scale = jnp.sum(arrived_weight.astype(jnp.float32) * pick[None, None, :], axis=2).reshape(
        node_count * capacity
    )
    weighted = (slice_out * slot_scale[:, None]).reshape(node_count, capacity, half_width)
    grouped = lax.psum_scatter(weighted, "local", scatter_dimension=2, tiled=True)
    returned = lax.all_to_all(grouped, "node", split_axis=0, concat_axis=0, tiled=True)
    partial_value = jnp.einsum("tmc,mcd->td", dispatch, returned, precision=lax.Precision.HIGHEST)
    summed = lax.all_to_all(partial_value, "local", split_axis=0, concat_axis=1, tiled=True)
    return summed.astype(jnp.bfloat16)


def on_device(tokens, expert_ids, affinity, w_gate, w_up, w_down):
    node_count = lax.axis_size("node")
    local_count = lax.axis_size("local")
    tok_count, top_count = expert_ids.shape
    expert_count = 2 * node_count
    capacity = (5 * tok_count * top_count + 4 * expert_count - 1) // (4 * expert_count)
    powers = all(size & (size - 1) == 0 for size in (node_count, local_count))
    everywhere = node_count == top_count // 2 and capacity >= tok_count and expert_count <= LANES
    chosen = dense_on_device if everywhere and powers and tok_count % local_count == 0 else slots_on_device
    return chosen(tokens, expert_ids, affinity, w_gate, w_up, w_down)


def solution(mesh):
    return jax.shard_map(
        on_device,
        mesh=mesh,
        in_specs=(
            P("node", "cuts"),
            P("node", None),
            P("node", None),
            P(("node", "local"), "cuts", None),
            P(("node", "local"), "cuts", None),
            P(("node", "local"), None, "cuts"),
        ),
        out_specs=P(("node", "local"), "cuts"),
        check_vma=False,
    )
```

```python
import jax
import jax.numpy as jnp
from jax import lax
from jax.experimental import pallas as pl
from jax.experimental.pallas import tpu as pltpu
from jax.sharding import PartitionSpec as P

LANES = 128


def swap(value, axis, bits):
    size = lax.axis_size(axis)
    return lax.ppermute(value, axis, [(i, i ^ bits) for i in range(size)])


def route_shares(affinity):
    affinity_sum = jnp.sum(affinity, axis=1, keepdims=True)
    return (2.5 * affinity / affinity_sum).astype(jnp.bfloat16).astype(jnp.float32)


def in_vmem(body, out_shapes, cost, *args):
    return pl.pallas_call(
        body,
        out_shape=out_shapes,
        in_specs=[pl.BlockSpec(memory_space=pltpu.VMEM)] * len(args),
        out_specs=jax.tree.map(lambda _: pl.BlockSpec(memory_space=pltpu.VMEM), out_shapes),
        compiler_params=pltpu.CompilerParams(vmem_limit_bytes=24 * 2**20),
        cost_estimate=pl.CostEstimate(flops=cost, bytes_accessed=2**20, transcendentals=0),
    )(*args)


def in_hbm(value):
    return pltpu.with_memory_space_constraint(value, pltpu.HBM)


def shape(*dims):
    return jax.ShapeDtypeStruct(dims, jnp.bfloat16)


def prepare(tokens, expert_ids, affinity, rows):
    tok_count, width = tokens.shape
    choices = expert_ids.shape[1]

    parts = tok_count // rows

    def body(tokens_hbm, ids_hbm, affinity_hbm, all_ref, share_ref, opposite_ref, ids_ref, affinity_ref, sems):
        copies = [
            pltpu.make_async_copy(tokens_hbm, all_ref.at[:, :width], sems.at[0]),
            pltpu.make_async_copy(ids_hbm, ids_ref, sems.at[1]),
            pltpu.make_async_copy(affinity_hbm, affinity_ref, sems.at[2]),
        ]
        for copy in copies:
            copy.start()
        copies[1].wait()
        copies[2].wait()
        total = jnp.sum(affinity_ref[...], axis=0, keepdims=True)
        share = (2.5 * affinity_ref[...] / total).astype(jnp.bfloat16).astype(jnp.float32)
        ids = ids_ref[...]
        lane = lax.broadcasted_iota(jnp.int32, (LANES, tok_count), 0)
        weight = jnp.zeros((LANES, tok_count), jnp.float32)
        for c in range(choices):
            weight += jnp.where(ids[c : c + 1, :] == lane, share[c : c + 1, :], 0.0)
        all_ref[:, width:] = weight.T.astype(jnp.bfloat16)
        copies[0].wait()
        for i in range(parts):
            other = i ^ (parts - 1)

            @pl.when(lax.axis_index("local") == i)
            def _():
                share_ref[...] = all_ref[i * rows : (i + 1) * rows, :]
                opposite_ref[...] = all_ref[other * rows : (other + 1) * rows, :]

    return pl.pallas_call(
        body,
        out_shape=(shape(tok_count, width + LANES), *[shape(rows, width + LANES)] * 2),
        in_specs=[pl.BlockSpec(memory_space=pltpu.HBM)] * 3,
        out_specs=[pl.BlockSpec(memory_space=pltpu.VMEM)] * 3,
        scratch_shapes=[
            pltpu.VMEM((choices, tok_count), jnp.int32),
            pltpu.VMEM((choices, tok_count), jnp.float32),
            pltpu.SemaphoreType.DMA((3,)),
        ],
        compiler_params=pltpu.CompilerParams(vmem_limit_bytes=24 * 2**20),
        cost_estimate=pl.CostEstimate(flops=10**6, bytes_accessed=2**20, transcendentals=0),
    )(*(in_hbm(value) for value in (tokens, expert_ids.T, affinity.T)))


def project_into(out_ref, rows, weight_refs, copies=()):
    hid = weight_refs[0].shape[1]
    for i, ref in enumerate(weight_refs):
        if copies:
            copies[i].wait()
        part = jnp.dot(rows, ref[...], preferred_element_type=jnp.float32)
        out_ref[:, i * hid : (i + 1) * hid] = part.astype(jnp.bfloat16)


def project(x, w_gate, w_up):
    count = x.shape[0]
    width, hid = w_gate.shape

    def body(x_ref, gate_ref, up_ref, out_ref):
        project_into(out_ref, x_ref[:, :width], (gate_ref, up_ref))

    return in_vmem(body, shape(count, 2 * hid), 4 * count * width * hid, x, w_gate, w_up)


def load_and_project(x, *weights):
    count = x.shape[0]
    width, hid = weights[0].shape

    def body(x_ref, gate_hbm, up_hbm, down_hbm, out_ref, gate_ref, up_ref, down_ref, sems):
        pairs = ((gate_hbm, gate_ref), (up_hbm, up_ref), (down_hbm, down_ref))
        copies = [pltpu.make_async_copy(src, dst, sems.at[i]) for i, (src, dst) in enumerate(pairs)]
        for copy in copies:
            copy.start()
        project_into(out_ref, x_ref[:, :width], (gate_ref, up_ref), copies)
        copies[2].wait()

    return pl.pallas_call(
        body,
        out_shape=(shape(count, 2 * hid), *(shape(*w.shape) for w in weights)),
        in_specs=[pl.BlockSpec(memory_space=pltpu.VMEM)] + [pl.BlockSpec(memory_space=pltpu.HBM)] * 3,
        out_specs=[pl.BlockSpec(memory_space=pltpu.VMEM)] * 4,
        scratch_shapes=[pltpu.SemaphoreType.DMA((3,))],
        compiler_params=pltpu.CompilerParams(vmem_limit_bytes=24 * 2**20),
    )(x, *(in_hbm(w) for w in weights))


def finish(x, part, other, w_down, group_size):
    count = x.shape[0]
    hid, width = w_down.shape

    def body(x_ref, part_ref, other_ref, down_ref, out_ref):
        both = part_ref[...].astype(jnp.float32) + other_ref[...].astype(jnp.float32)
        gate, up = both[:, :hid], both[:, hid:]
        hidden = (gate / (1.0 + jnp.exp(-gate)) * up).astype(jnp.bfloat16)
        expert = 2 * lax.axis_index("node") + lax.axis_index("local") // group_size
        lane = lax.broadcasted_iota(jnp.int32, (count, LANES), 1)
        table = x_ref[:, width:].astype(jnp.float32)
        scale = jnp.sum(jnp.where(lane == expert, table, 0.0), axis=1, keepdims=True)
        out = jnp.dot(hidden, down_ref[...], preferred_element_type=jnp.float32)
        out_ref[...] = (out * scale).astype(jnp.bfloat16)

    return in_vmem(body, shape(count, width), 2 * count * width * hid, x, part, other, w_down)


def merge(rows, partners, *values):
    count, width = values[0].shape
    parts = count // rows

    def body(own_ref, near_ref, direct_ref, *out_refs):
        for i in range(parts):

            @pl.when(lax.axis_index("local") == i)
            def _():
                for j, ref in zip((0, *partners), out_refs):
                    where = pl.ds((i ^ j) * rows, rows)
                    total = own_ref[where, :].astype(jnp.float32) + near_ref[where, :].astype(jnp.float32)
                    if j == parts - 1:
                        total += direct_ref[...].astype(jnp.float32)
                    ref[...] = total.astype(jnp.bfloat16)

    return in_vmem(body, tuple(shape(rows, width) for _ in range(parts)), 3 * count * width, *values)


def after(value, *others):
    return lax.optimization_barrier((value, *others))[0]


def dense_on_device(tokens, expert_ids, affinity, w_gate, w_up, w_down):
    node_count = lax.axis_size("node")
    local_count = lax.axis_size("local")
    group_size = local_count // 2
    tok_count, _ = expert_ids.shape
    rows = tok_count // local_count
    far = list(range(node_count - 1, 1, -1))

    def split(value):
        step = value.shape[0] // local_count
        return [value[j * step : (j + 1) * step] for j in range(local_count)]

    everything, own, opposite = prepare(tokens, expert_ids, affinity, rows)
    arrived = {k: swap(own, "node", k) for k in far}
    near = swap(everything, "node", 1)
    part_own, gate, up, down = load_and_project(everything, w_gate[0], w_up[0], w_down[0])

    def begin(x):
        part = project(x, gate, up)
        return x, part, swap(part, "cuts", 1)

    def complete(state, *others):
        x, part, other = state
        return finish(x, part, after(other, *others), down, group_size)

    gather_order = sorted(range(1, local_count), key=lambda j: (j.bit_count(), -j))
    sum_order = sorted(range(1, local_count), key=lambda j: (-j.bit_count(), j))

    def exchanged(blocks, order):
        return [swap(block, "local", j) for j, block in zip(order, blocks)]

    def summed(values):
        return sum(value.astype(jnp.float32) for value in values)

    arrived[far[0]] = after(arrived[far[0]], part_own)
    joined = jnp.concatenate([arrived[k] for k in far], axis=0)
    fewer = jnp.concatenate([arrived[k] for k in far[:-1]], axis=0)
    others = exchanged([fewer if j == local_count - 1 else joined for j in gather_order], gather_order)
    out_own = complete((everything, part_own, swap(part_own, "cuts", 1)))
    direct = swap(after(opposite, *arrived.values()), "node", far[-1])
    near_state = begin(near)
    out_near = complete(near_state)
    others[1] = after(others[1], near_state[1])
    others[2] = after(others[2], out_near)
    by_partner = [joined] + [others[gather_order.index(j)] for j in range(1, local_count)] + [direct]
    state = begin(after(jnp.concatenate(by_partner, axis=0), out_own))
    near_back = swap(out_near, "node", 1)
    out_far = complete(state, out_near)
    blocks = split(out_far)
    direct_back = swap(blocks[-1][-rows:], "node", far[-1])
    blocks[-1] = blocks[-1][:-rows]
    got = dict(zip(sum_order, exchanged([blocks[j] for j in sum_order], sum_order)))
    def piece(j, i):
        return got[j][i * rows : (i + 1) * rows]

    begun = summed([blocks[0][:-rows], got[local_count - 1]])
    rest = [j for j in sum_order if j != local_count - 1]
    begun, *values = lax.optimization_barrier((begun, *[got[j] for j in rest]))
    got.update(zip(rest, values))
    done = [begun[i * rows : (i + 1) * rows] for i in range(len(far) - 1)] + [blocks[0][-rows:].astype(jnp.float32)]
    done = [(value + summed([piece(j, i) for j in rest])).astype(jnp.bfloat16) for i, value in enumerate(done)]
    back = [swap(value, "node", k) for value, k in zip(done, far)]
    out_own = after(out_own, *done)
    mine, *blocks = merge(rows, sum_order, out_own, near_back, direct_back)
    later = exchanged(blocks, sum_order)
    total, *later = lax.optimization_barrier((summed(back), *later))
    return (total + summed([mine, *later])).astype(jnp.bfloat16)


def slots_on_device(tokens, expert_ids, affinity, w_gate, w_up, w_down):
    node_count = lax.axis_size("node")
    local_count = lax.axis_size("local")
    group_size = local_count // 2
    expert_count = 2 * node_count
    tok_count, top_count = expert_ids.shape
    capacity = (5 * tok_count * top_count + 4 * expert_count - 1) // (4 * expert_count)
    half_width = tokens.shape[1]
    my_local = lax.axis_index("local")
    pair_index = my_local // group_size
    node_range = jnp.arange(node_count, dtype=jnp.int32)
    chosen_node = jnp.any(
        (expert_ids // 2)[:, :, None] == node_range[None, None, :], axis=1
    ).astype(jnp.float32)
    tok_range = jnp.arange(tok_count, dtype=jnp.int32)
    earlier = (tok_range[None, :] < tok_range[:, None]).astype(jnp.float32)
    node_rank = jnp.dot(earlier, chosen_node, precision=lax.Precision.HIGHEST)
    slot_range = jnp.arange(capacity, dtype=jnp.float32)
    dispatch = chosen_node[:, :, None] * (
        node_rank[:, :, None] == slot_range[None, None, :]
    ).astype(jnp.float32)
    outgoing = jnp.einsum(
        "tmc,td->mcd", dispatch.astype(jnp.bfloat16), tokens, preferred_element_type=jnp.float32
    ).astype(jnp.bfloat16)
    route_share = route_shares(affinity)
    pair_range = jnp.arange(2, dtype=jnp.int32)
    expert_grid = 2 * node_range[:, None] + pair_range[None, :]
    own_route = expert_ids[:, :, None, None] == expert_grid[None, None, :, :]
    pair_weight = jnp.sum(jnp.where(own_route, route_share[:, :, None, None], 0.0), axis=1)
    slot_weight = jnp.einsum(
        "tmc,tmp->mcp", dispatch, pair_weight, precision=lax.Precision.HIGHEST
    ).astype(jnp.bfloat16)
    arrived, arrived_weight = (
        lax.all_to_all(outgoing, "node", split_axis=0, concat_axis=0, tiled=True),
        lax.all_to_all(slot_weight, "node", split_axis=0, concat_axis=0, tiled=True),
    )
    expert_rows = arrived.reshape(node_count * capacity, half_width)
    gate_part = jnp.dot(expert_rows, w_gate[0], preferred_element_type=jnp.float32)
    up_part = jnp.dot(expert_rows, w_up[0], preferred_element_type=jnp.float32)
    gate_full, up_full = lax.psum((gate_part, up_part), "cuts")
    hidden = (jax.nn.silu(gate_full) * up_full).astype(jnp.bfloat16)
    slice_out = jnp.dot(hidden, w_down[0], preferred_element_type=jnp.float32)
    pick = (pair_range == pair_index).astype(jnp.float32)
    slot_scale = jnp.sum(arrived_weight.astype(jnp.float32) * pick[None, None, :], axis=2).reshape(
        node_count * capacity
    )
    weighted = (slice_out * slot_scale[:, None]).reshape(node_count, capacity, half_width)
    grouped = lax.psum_scatter(weighted, "local", scatter_dimension=2, tiled=True)
    returned = lax.all_to_all(grouped, "node", split_axis=0, concat_axis=0, tiled=True)
    partial_value = jnp.einsum("tmc,mcd->td", dispatch, returned, precision=lax.Precision.HIGHEST)
    summed = lax.all_to_all(partial_value, "local", split_axis=0, concat_axis=1, tiled=True)
    return summed.astype(jnp.bfloat16)


def on_device(tokens, expert_ids, affinity, w_gate, w_up, w_down):
    node_count = lax.axis_size("node")
    local_count = lax.axis_size("local")
    tok_count, top_count = expert_ids.shape
    expert_count = 2 * node_count
    capacity = (5 * tok_count * top_count + 4 * expert_count - 1) // (4 * expert_count)
    powers = all(size & (size - 1) == 0 for size in (node_count, local_count))
    everywhere = node_count == top_count // 2 and capacity >= tok_count and expert_count <= LANES
    everywhere = everywhere and node_count > 2 and local_count > 2
    chosen = dense_on_device if everywhere and powers and tok_count % local_count == 0 else slots_on_device
    return chosen(tokens, expert_ids, affinity, w_gate, w_up, w_down)


def solution(mesh):
    return jax.shard_map(
        on_device,
        mesh=mesh,
        in_specs=(
            P("node", "cuts"),
            P("node", None),
            P("node", None),
            P(("node", "local"), "cuts", None),
            P(("node", "local"), "cuts", None),
            P(("node", "local"), None, "cuts"),
        ),
        out_specs=P(("node", "local"), "cuts"),
        check_vma=False,
    )
```

```python
import jax
import jax.numpy as jnp
from jax import lax
from jax.experimental import pallas as pl
from jax.experimental.pallas import tpu as pltpu
from jax.sharding import PartitionSpec as P

LANES = 128


def swap(value, axis, bits):
    size = lax.axis_size(axis)
    return lax.ppermute(value, axis, [(i, i ^ bits) for i in range(size)])


def route_shares(affinity):
    affinity_sum = jnp.sum(affinity, axis=1, keepdims=True)
    return (2.5 * affinity / affinity_sum).astype(jnp.bfloat16).astype(jnp.float32)


def in_vmem(body, out_shapes, cost, *args):
    return pl.pallas_call(
        body,
        out_shape=out_shapes,
        in_specs=[pl.BlockSpec(memory_space=pltpu.VMEM)] * len(args),
        out_specs=jax.tree.map(lambda _: pl.BlockSpec(memory_space=pltpu.VMEM), out_shapes),
        compiler_params=pltpu.CompilerParams(vmem_limit_bytes=24 * 2**20),
        cost_estimate=pl.CostEstimate(flops=cost, bytes_accessed=2**20, transcendentals=0),
    )(*args)


def in_hbm(value):
    return pltpu.with_memory_space_constraint(value, pltpu.HBM)


def shape(*dims):
    return jax.ShapeDtypeStruct(dims, jnp.bfloat16)


def prepare(tokens, expert_ids, affinity, rows):
    tok_count, width = tokens.shape
    choices = expert_ids.shape[1]

    parts = tok_count // rows

    def body(tokens_hbm, ids_hbm, affinity_hbm, all_ref, share_ref, opposite_ref, ids_ref, affinity_ref, sems):
        copies = [
            pltpu.make_async_copy(tokens_hbm, all_ref.at[:, :width], sems.at[0]),
            pltpu.make_async_copy(ids_hbm, ids_ref, sems.at[1]),
            pltpu.make_async_copy(affinity_hbm, affinity_ref, sems.at[2]),
        ]
        for copy in copies:
            copy.start()
        copies[1].wait()
        copies[2].wait()
        total = jnp.sum(affinity_ref[...], axis=0, keepdims=True)
        share = (2.5 * affinity_ref[...] / total).astype(jnp.bfloat16).astype(jnp.float32)
        ids = ids_ref[...]
        lane = lax.broadcasted_iota(jnp.int32, (LANES, tok_count), 0)
        weight = jnp.zeros((LANES, tok_count), jnp.float32)
        for c in range(choices):
            weight += jnp.where(ids[c : c + 1, :] == lane, share[c : c + 1, :], 0.0)
        all_ref[:, width:] = weight.T.astype(jnp.bfloat16)
        copies[0].wait()
        for i in range(parts):
            other = i ^ (parts - 1)

            @pl.when(lax.axis_index("local") == i)
            def _():
                share_ref[...] = all_ref[i * rows : (i + 1) * rows, :]
                opposite_ref[...] = all_ref[other * rows : (other + 1) * rows, :]

    return pl.pallas_call(
        body,
        out_shape=(shape(tok_count, width + LANES), *[shape(rows, width + LANES)] * 2),
        in_specs=[pl.BlockSpec(memory_space=pltpu.HBM)] * 3,
        out_specs=[pl.BlockSpec(memory_space=pltpu.VMEM)] * 3,
        scratch_shapes=[
            pltpu.VMEM((choices, tok_count), jnp.int32),
            pltpu.VMEM((choices, tok_count), jnp.float32),
            pltpu.SemaphoreType.DMA((3,)),
        ],
        compiler_params=pltpu.CompilerParams(vmem_limit_bytes=24 * 2**20),
        cost_estimate=pl.CostEstimate(flops=10**6, bytes_accessed=2**20, transcendentals=0),
    )(*(in_hbm(value) for value in (tokens, expert_ids.T, affinity.T)))


def project_into(out_ref, rows, weight_refs, copies=()):
    hid = weight_refs[0].shape[1]
    for i, ref in enumerate(weight_refs):
        if copies:
            copies[i].wait()
        part = jnp.dot(rows, ref[...], preferred_element_type=jnp.float32)
        out_ref[:, i * hid : (i + 1) * hid] = part.astype(jnp.bfloat16)


def project(x, w_gate, w_up):
    count = x.shape[0]
    width, hid = w_gate.shape

    def body(x_ref, gate_ref, up_ref, out_ref):
        project_into(out_ref, x_ref[:, :width], (gate_ref, up_ref))

    return in_vmem(body, shape(count, 2 * hid), 4 * count * width * hid, x, w_gate, w_up)


def load_and_project(x, *weights):
    count = x.shape[0]
    width, hid = weights[0].shape

    def body(x_ref, gate_hbm, up_hbm, down_hbm, out_ref, gate_ref, up_ref, down_ref, sems):
        pairs = ((gate_hbm, gate_ref), (up_hbm, up_ref), (down_hbm, down_ref))
        copies = [pltpu.make_async_copy(src, dst, sems.at[i]) for i, (src, dst) in enumerate(pairs)]
        for copy in copies:
            copy.start()
        project_into(out_ref, x_ref[:, :width], (gate_ref, up_ref), copies)
        copies[2].wait()

    return pl.pallas_call(
        body,
        out_shape=(shape(count, 2 * hid), *(shape(*w.shape) for w in weights)),
        in_specs=[pl.BlockSpec(memory_space=pltpu.VMEM)] + [pl.BlockSpec(memory_space=pltpu.HBM)] * 3,
        out_specs=[pl.BlockSpec(memory_space=pltpu.VMEM)] * 4,
        scratch_shapes=[pltpu.SemaphoreType.DMA((3,))],
        compiler_params=pltpu.CompilerParams(vmem_limit_bytes=24 * 2**20),
    )(x, *(in_hbm(w) for w in weights))


def finish(x, part, other, w_down, group_size):
    count = x.shape[0]
    hid, width = w_down.shape

    def body(x_ref, part_ref, other_ref, down_ref, out_ref):
        both = part_ref[...].astype(jnp.float32) + other_ref[...].astype(jnp.float32)
        gate, up = both[:, :hid], both[:, hid:]
        hidden = (gate / (1.0 + jnp.exp(-gate)) * up).astype(jnp.bfloat16)
        expert = 2 * lax.axis_index("node") + lax.axis_index("local") // group_size
        lane = lax.broadcasted_iota(jnp.int32, (count, LANES), 1)
        table = x_ref[:, width:].astype(jnp.float32)
        scale = jnp.sum(jnp.where(lane == expert, table, 0.0), axis=1, keepdims=True)
        out = jnp.dot(hidden, down_ref[...], preferred_element_type=jnp.float32)
        out_ref[...] = (out * scale).astype(jnp.bfloat16)

    return in_vmem(body, shape(count, width), 2 * count * width * hid, x, part, other, w_down)


def merge(rows, partners, *values):
    count, width = values[0].shape
    parts = count // rows

    def body(own_ref, near_ref, direct_ref, *out_refs):
        for i in range(parts):

            @pl.when(lax.axis_index("local") == i)
            def _():
                for j, ref in zip((0, *partners), out_refs):
                    where = pl.ds((i ^ j) * rows, rows)
                    total = own_ref[where, :].astype(jnp.float32) + near_ref[where, :].astype(jnp.float32)
                    if j == parts - 1:
                        total += direct_ref[...].astype(jnp.float32)
                    ref[...] = total.astype(jnp.bfloat16)

    return in_vmem(body, tuple(shape(rows, width) for _ in range(parts)), 3 * count * width, *values)


def after(value, *others):
    return lax.optimization_barrier((value, *others))[0]


def dense_on_device(tokens, expert_ids, affinity, w_gate, w_up, w_down):
    node_count = lax.axis_size("node")
    local_count = lax.axis_size("local")
    group_size = local_count // 2
    tok_count, _ = expert_ids.shape
    rows = tok_count // local_count
    far = list(range(node_count - 1, 1, -1))

    def split(value):
        step = value.shape[0] // local_count
        return [value[j * step : (j + 1) * step] for j in range(local_count)]

    everything, own, opposite = prepare(tokens, expert_ids, affinity, rows)
    near = swap(everything, "node", 1)
    arrived = {k: swap(own, "node", k) for k in far}
    part_own, gate, up, down = load_and_project(everything, w_gate[0], w_up[0], w_down[0])

    def begin(x):
        part = project(x, gate, up)
        return x, part, swap(part, "cuts", 1)

    def complete(state, *others):
        x, part, other = state
        return finish(x, part, after(other, *others), down, group_size)

    sum_order = list(range(1, local_count))
    gather_order = sorted(sum_order, key=lambda j: (-j.bit_count(), j))

    def exchanged(blocks, order):
        return [swap(block, "local", j) for j, block in zip(order, blocks)]

    def summed(values):
        return sum(value.astype(jnp.float32) for value in values)

    arrived[far[0]] = after(arrived[far[0]], part_own)
    joined = jnp.concatenate([arrived[k] for k in far], axis=0)
    fewer = jnp.concatenate([arrived[k] for k in far[:-1]], axis=0)
    others = exchanged([fewer if j == local_count - 1 else joined for j in gather_order], gather_order)
    out_own = complete((everything, part_own, swap(part_own, "cuts", 1)))
    direct = swap(after(opposite, *arrived.values()), "node", far[-1])
    near_state = begin(after(near, out_own))
    out_near = complete(near_state)
    others[1] = after(others[1], near_state[1])
    others[2] = after(others[2], out_near)
    by_partner = [joined] + [others[gather_order.index(j)] for j in range(1, local_count)] + [direct]
    state = begin(jnp.concatenate(by_partner, axis=0))
    near_back = swap(out_near, "node", 1)
    out_far = complete(state, out_near)
    blocks = split(out_far)
    direct_back = swap(after(blocks[-1][-rows:], out_near), "node", far[-1])
    blocks[-1] = blocks[-1][:-rows]
    got = dict(zip(sum_order, exchanged([blocks[j] for j in sum_order], sum_order)))

    def piece(j, i):
        return got[j][i * rows : (i + 1) * rows]

    begun = summed([blocks[0][:-rows], got[local_count - 1]])
    rest = [j for j in sum_order if j != local_count - 1]
    begun, *values = lax.optimization_barrier((begun, *[got[j] for j in rest]))
    got.update(zip(rest, values))
    done = [begun[i * rows : (i + 1) * rows] for i in range(len(far) - 1)] + [blocks[0][-rows:].astype(jnp.float32)]
    done = [(value + summed([piece(j, i) for j in rest])).astype(jnp.bfloat16) for i, value in enumerate(done)]
    back = [swap(value, "node", k) for value, k in zip(done, far)]
    out_own = after(out_own, *done)
    mine, *blocks = merge(rows, gather_order, out_own, near_back, direct_back)
    later = exchanged(blocks, gather_order)
    *back, last = back
    total = summed([*back, mine])
    total, *later = lax.optimization_barrier((total, *later))
    total, last = lax.optimization_barrier((total + summed(later), last))
    return (total + last.astype(jnp.float32)).astype(jnp.bfloat16)


def slots_on_device(tokens, expert_ids, affinity, w_gate, w_up, w_down):
    node_count = lax.axis_size("node")
    local_count = lax.axis_size("local")
    group_size = local_count // 2
    expert_count = 2 * node_count
    tok_count, top_count = expert_ids.shape
    capacity = (5 * tok_count * top_count + 4 * expert_count - 1) // (4 * expert_count)
    half_width = tokens.shape[1]
    my_local = lax.axis_index("local")
    pair_index = my_local // group_size
    node_range = jnp.arange(node_count, dtype=jnp.int32)
    chosen_node = jnp.any(
        (expert_ids // 2)[:, :, None] == node_range[None, None, :], axis=1
    ).astype(jnp.float32)
    tok_range = jnp.arange(tok_count, dtype=jnp.int32)
    earlier = (tok_range[None, :] < tok_range[:, None]).astype(jnp.float32)
    node_rank = jnp.dot(earlier, chosen_node, precision=lax.Precision.HIGHEST)
    slot_range = jnp.arange(capacity, dtype=jnp.float32)
    dispatch = chosen_node[:, :, None] * (
        node_rank[:, :, None] == slot_range[None, None, :]
    ).astype(jnp.float32)
    outgoing = jnp.einsum(
        "tmc,td->mcd", dispatch.astype(jnp.bfloat16), tokens, preferred_element_type=jnp.float32
    ).astype(jnp.bfloat16)
    route_share = route_shares(affinity)
    pair_range = jnp.arange(2, dtype=jnp.int32)
    expert_grid = 2 * node_range[:, None] + pair_range[None, :]
    own_route = expert_ids[:, :, None, None] == expert_grid[None, None, :, :]
    pair_weight = jnp.sum(jnp.where(own_route, route_share[:, :, None, None], 0.0), axis=1)
    slot_weight = jnp.einsum(
        "tmc,tmp->mcp", dispatch, pair_weight, precision=lax.Precision.HIGHEST
    ).astype(jnp.bfloat16)
    arrived, arrived_weight = (
        lax.all_to_all(outgoing, "node", split_axis=0, concat_axis=0, tiled=True),
        lax.all_to_all(slot_weight, "node", split_axis=0, concat_axis=0, tiled=True),
    )
    expert_rows = arrived.reshape(node_count * capacity, half_width)
    gate_part = jnp.dot(expert_rows, w_gate[0], preferred_element_type=jnp.float32)
    up_part = jnp.dot(expert_rows, w_up[0], preferred_element_type=jnp.float32)
    gate_full, up_full = lax.psum((gate_part, up_part), "cuts")
    hidden = (jax.nn.silu(gate_full) * up_full).astype(jnp.bfloat16)
    slice_out = jnp.dot(hidden, w_down[0], preferred_element_type=jnp.float32)
    pick = (pair_range == pair_index).astype(jnp.float32)
    slot_scale = jnp.sum(arrived_weight.astype(jnp.float32) * pick[None, None, :], axis=2).reshape(
        node_count * capacity
    )
    weighted = (slice_out * slot_scale[:, None]).reshape(node_count, capacity, half_width)
    grouped = lax.psum_scatter(weighted, "local", scatter_dimension=2, tiled=True)
    returned = lax.all_to_all(grouped, "node", split_axis=0, concat_axis=0, tiled=True)
    partial_value = jnp.einsum("tmc,mcd->td", dispatch, returned, precision=lax.Precision.HIGHEST)
    summed = lax.all_to_all(partial_value, "local", split_axis=0, concat_axis=1, tiled=True)
    return summed.astype(jnp.bfloat16)


def on_device(tokens, expert_ids, affinity, w_gate, w_up, w_down):
    node_count = lax.axis_size("node")
    local_count = lax.axis_size("local")
    tok_count, top_count = expert_ids.shape
    expert_count = 2 * node_count
    capacity = (5 * tok_count * top_count + 4 * expert_count - 1) // (4 * expert_count)
    powers = all(size & (size - 1) == 0 for size in (node_count, local_count))
    everywhere = node_count == top_count // 2 and capacity >= tok_count and expert_count <= LANES
    everywhere = everywhere and node_count > 2 and local_count > 2
    chosen = dense_on_device if everywhere and powers and tok_count % local_count == 0 else slots_on_device
    return chosen(tokens, expert_ids, affinity, w_gate, w_up, w_down)


def solution(mesh):
    return jax.shard_map(
        on_device,
        mesh=mesh,
        in_specs=(
            P("node", "cuts"),
            P("node", None),
            P("node", None),
            P(("node", "local"), "cuts", None),
            P(("node", "local"), "cuts", None),
            P(("node", "local"), None, "cuts"),
        ),
        out_specs=P(("node", "local"), "cuts"),
        check_vma=False,
    )
```

```python
import jax
import jax.numpy as jnp
from jax import lax
from jax.experimental import pallas as pl
from jax.experimental.pallas import tpu as pltpu
from jax.sharding import PartitionSpec as P

LANES = 128


def swap(value, axis, bits):
    size = lax.axis_size(axis)
    return lax.ppermute(value, axis, [(i, i ^ bits) for i in range(size)])


def route_shares(affinity):
    affinity_sum = jnp.sum(affinity, axis=1, keepdims=True)
    return (2.5 * affinity / affinity_sum).astype(jnp.bfloat16).astype(jnp.float32)


def in_vmem(body, out_shapes, cost, *args):
    return pl.pallas_call(
        body,
        out_shape=out_shapes,
        in_specs=[pl.BlockSpec(memory_space=pltpu.VMEM)] * len(args),
        out_specs=jax.tree.map(lambda _: pl.BlockSpec(memory_space=pltpu.VMEM), out_shapes),
        compiler_params=pltpu.CompilerParams(vmem_limit_bytes=24 * 2**20),
        cost_estimate=pl.CostEstimate(flops=cost, bytes_accessed=2**20, transcendentals=0),
    )(*args)


def in_hbm(value):
    return pltpu.with_memory_space_constraint(value, pltpu.HBM)


def shape(*dims):
    return jax.ShapeDtypeStruct(dims, jnp.bfloat16)


def prepare(tokens, expert_ids, affinity, rows, expert_count):
    tok_count, width = tokens.shape
    choices = expert_ids.shape[1]
    parts = tok_count // rows

    def body(tokens_hbm, ids_hbm, affinity_hbm, all_ref, share_ref, opposite_ref, ids_ref, affinity_ref, sems):
        copies = [
            pltpu.make_async_copy(tokens_hbm, all_ref.at[:, :width], sems.at[0]),
            pltpu.make_async_copy(ids_hbm, ids_ref, sems.at[1]),
            pltpu.make_async_copy(affinity_hbm, affinity_ref, sems.at[2]),
        ]
        for copy in copies:
            copy.start()
        copies[1].wait()
        copies[2].wait()
        total = jnp.sum(affinity_ref[...], axis=0, keepdims=True)
        share = (2.5 * affinity_ref[...] / total).astype(jnp.bfloat16).astype(jnp.float32)
        ids = ids_ref[...]
        lane = lax.broadcasted_iota(jnp.int32, (LANES, tok_count), 0)
        weight = jnp.zeros((LANES, tok_count), jnp.float32)
        for c in range(choices):
            weight += jnp.where(ids[c : c + 1, :] == lane, share[c : c + 1, :], 0.0)
        weight = weight.T
        all_ref[:, width:] = weight.astype(jnp.bfloat16)
        copies[0].wait()
        for i in range(parts):
            opposite = i ^ (parts - 1)

            @pl.when(lax.axis_index("local") == i)
            def _():
                lanes = jnp.zeros((rows, LANES), jnp.float32)
                for j in range(parts):
                    mine = weight[(i ^ j) * rows : ((i ^ j) + 1) * rows, :]
                    lanes += mine if j == 0 else pltpu.roll(mine, j * expert_count, 1)
                share_ref[:, :width] = all_ref[i * rows : (i + 1) * rows, :width]
                share_ref[:, width:] = lanes.astype(jnp.bfloat16)
                opposite_ref[...] = all_ref[opposite * rows : (opposite + 1) * rows, :width]

    return pl.pallas_call(
        body,
        out_shape=(shape(tok_count, width + LANES), shape(rows, width + LANES), shape(rows, width)),
        in_specs=[pl.BlockSpec(memory_space=pltpu.HBM)] * 3,
        out_specs=[pl.BlockSpec(memory_space=pltpu.VMEM)] * 3,
        scratch_shapes=[
            pltpu.VMEM((choices, tok_count), jnp.int32),
            pltpu.VMEM((choices, tok_count), jnp.float32),
            pltpu.SemaphoreType.DMA((3,)),
        ],
        compiler_params=pltpu.CompilerParams(vmem_limit_bytes=24 * 2**20),
        cost_estimate=pl.CostEstimate(flops=10**6, bytes_accessed=2**20, transcendentals=0),
    )(*(in_hbm(value) for value in (tokens, expert_ids.T, affinity.T)))


def project_into(out_ref, rows, weight_refs, copies=()):
    hid = weight_refs[0].shape[1]
    for i, ref in enumerate(weight_refs):
        if copies:
            copies[i].wait()
        part = jnp.dot(rows, ref[...], preferred_element_type=jnp.float32)
        out_ref[:, i * hid : (i + 1) * hid] = part.astype(jnp.bfloat16)


def project(pieces, w_gate, w_up):
    counts = [piece.shape[0] for piece in pieces]
    width, hid = w_gate.shape

    def body(*refs):
        *piece_refs, gate_ref, up_ref, out_ref = refs
        rows = jnp.concatenate([ref[:, :width] for ref in piece_refs], axis=0)
        project_into(out_ref, rows, (gate_ref, up_ref))

    return in_vmem(body, shape(sum(counts), 2 * hid), 4 * sum(counts) * width * hid, *pieces, w_gate, w_up)


def load_and_project(x, *weights):
    count = x.shape[0]
    width, hid = weights[0].shape

    def body(x_ref, gate_hbm, up_hbm, down_hbm, out_ref, gate_ref, up_ref, down_ref, sems):
        pairs = ((gate_hbm, gate_ref), (up_hbm, up_ref), (down_hbm, down_ref))
        copies = [pltpu.make_async_copy(src, dst, sems.at[i]) for i, (src, dst) in enumerate(pairs)]
        for copy in copies:
            copy.start()
        project_into(out_ref, x_ref[:, :width], (gate_ref, up_ref), copies)
        copies[2].wait()

    return pl.pallas_call(
        body,
        out_shape=(shape(count, 2 * hid), *(shape(*w.shape) for w in weights)),
        in_specs=[pl.BlockSpec(memory_space=pltpu.VMEM)] + [pl.BlockSpec(memory_space=pltpu.HBM)] * 3,
        out_specs=[pl.BlockSpec(memory_space=pltpu.VMEM)] * 4,
        scratch_shapes=[pltpu.SemaphoreType.DMA((3,))],
        compiler_params=pltpu.CompilerParams(vmem_limit_bytes=24 * 2**20),
    )(x, *(in_hbm(w) for w in weights))


def finish(tables, layout, group_size, part, other, w_down):
    hid, width = w_down.shape
    counts = [sum(tables[t].shape[0] for t, _ in runs) for runs in layout]

    def body(*refs):
        table_refs = refs[: len(tables)]
        part_ref, other_ref, down_ref = refs[len(tables) : len(tables) + 3]
        out_refs = refs[len(tables) + 3 :]
        both = part_ref[...].astype(jnp.float32) + other_ref[...].astype(jnp.float32)
        gate, up = both[:, :hid], both[:, hid:]
        hidden = (gate / (1.0 + jnp.exp(-gate)) * up).astype(jnp.bfloat16)
        expert = 2 * lax.axis_index("node") + lax.axis_index("local") // group_size
        columns = []
        for runs in layout:
            for t, first in runs:
                table = table_refs[t][:, width:].astype(jnp.float32)
                lane = lax.broadcasted_iota(jnp.int32, table.shape, 1)
                columns.append(jnp.sum(jnp.where(lane == expert + first, table, 0.0), axis=1, keepdims=True))
        out = jnp.dot(hidden, down_ref[...], preferred_element_type=jnp.float32)
        out = (out * jnp.concatenate(columns, axis=0)).astype(jnp.bfloat16)
        start = 0
        for count, ref in zip(counts, out_refs):
            ref[...] = out[start : start + count, :]
            start += count

    outs = [shape(count, width) for count in counts]
    return in_vmem(body, outs, 2 * sum(counts) * width * hid, *tables, part, other, w_down)


def merge(rows, partners, *values):
    count, width = values[0].shape
    parts = count // rows

    def body(own_ref, near_ref, direct_ref, *out_refs):
        for i in range(parts):

            @pl.when(lax.axis_index("local") == i)
            def _():
                for j, ref in zip((0, *partners), out_refs):
                    where = pl.ds((i ^ j) * rows, rows)
                    total = own_ref[where, :].astype(jnp.float32) + near_ref[where, :].astype(jnp.float32)
                    if j == parts - 1:
                        total += direct_ref[...].astype(jnp.float32)
                    ref[...] = total.astype(jnp.bfloat16)

    return in_vmem(body, tuple(shape(rows, width) for _ in range(parts)), 3 * count * width, *values)


def after(value, *others):
    return lax.optimization_barrier((value, *others))[0]


def dense_on_device(tokens, expert_ids, affinity, w_gate, w_up, w_down):
    node_count = lax.axis_size("node")
    local_count = lax.axis_size("local")
    group_size = local_count // 2
    tok_count, _ = expert_ids.shape
    rows = tok_count // local_count
    width = tokens.shape[1]
    far = list(range(node_count - 1, 1, -1))

    def split(value):
        step = value.shape[0] // local_count
        return [value[j * step : (j + 1) * step] for j in range(local_count)]

    everything, own, opposite = prepare(tokens, expert_ids, affinity, rows, 2 * node_count)
    near = swap(everything, "node", 1)
    arrived = {k: swap(own, "node", k) for k in far}
    part_own, gate, up, down = load_and_project(everything, w_gate[0], w_up[0], w_down[0])

    def begin(x):
        part = project([x], gate, up)
        return x, part, swap(part, "cuts", 1)

    def complete(state, *others, tables=None, lanes=(0,)):
        x, part, other = state
        tables = [x] if tables is None else tables
        layout = [[(t, first) for first in lanes for t in range(len(tables))]]
        return finish(tables, layout, group_size, part, after(other, *others), down)[0]

    sum_order = list(range(1, local_count))
    gather_order = sorted(sum_order, key=lambda j: (-j.bit_count(), j))

    def exchanged(blocks, order):
        return [swap(block, "local", j) for j, block in zip(order, blocks)]

    def summed(values):
        return sum(value.astype(jnp.float32) for value in values)

    arrived[far[0]] = after(arrived[far[0]], part_own)
    joined = jnp.concatenate([arrived[k][:, :width] for k in far], axis=0)
    fewer = jnp.concatenate([arrived[k][:, :width] for k in far[:-1]], axis=0)
    others = exchanged([fewer if j == local_count - 1 else joined for j in gather_order], gather_order)
    out_own = complete((everything, part_own, swap(part_own, "cuts", 1)))
    direct = swap(after(opposite, *arrived.values()), "node", far[-1])
    near_state = begin(near)
    out_near = complete(near_state)
    others[1] = after(others[1], near_state[1])
    others[2] = after(others[2], out_near)
    by_partner = [joined] + [others[gather_order.index(j)] for j in range(1, local_count)] + [direct]
    state = begin(after(jnp.concatenate(by_partner, axis=0), out_own))
    near_back = swap(out_near, "node", 1)
    lanes = [2 * node_count * j for j in range(local_count)]
    out_far = complete(state, out_near, tables=[arrived[k] for k in far], lanes=lanes)
    blocks = split(out_far)
    direct_back = swap(after(blocks[-1][-rows:], out_near), "node", far[-1])
    blocks[-1] = blocks[-1][:-rows]
    got = dict(zip(sum_order, exchanged([blocks[j] for j in sum_order], sum_order)))

    def piece(j, i):
        return got[j][i * rows : (i + 1) * rows]

    begun = summed([blocks[0][:-rows], got[local_count - 1]])
    rest = [j for j in sum_order if j != local_count - 1]
    begun, *values = lax.optimization_barrier((begun, *[got[j] for j in rest]))
    got.update(zip(rest, values))
    done = [begun[i * rows : (i + 1) * rows] for i in range(len(far) - 1)] + [blocks[0][-rows:].astype(jnp.float32)]
    done = [(value + summed([piece(j, i) for j in rest])).astype(jnp.bfloat16) for i, value in enumerate(done)]
    back = [swap(value, "node", k) for value, k in zip(done, far)]
    out_own = after(out_own, *done)
    mine, *blocks = merge(rows, gather_order, out_own, near_back, direct_back)
    later = exchanged(blocks, gather_order)
    total, *later = lax.optimization_barrier((summed(back), *later))
    return (total + summed([mine, *later])).astype(jnp.bfloat16)


def slots_on_device(tokens, expert_ids, affinity, w_gate, w_up, w_down):
    node_count = lax.axis_size("node")
    local_count = lax.axis_size("local")
    group_size = local_count // 2
    expert_count = 2 * node_count
    tok_count, top_count = expert_ids.shape
    capacity = (5 * tok_count * top_count + 4 * expert_count - 1) // (4 * expert_count)
    half_width = tokens.shape[1]
    my_local = lax.axis_index("local")
    pair_index = my_local // group_size
    node_range = jnp.arange(node_count, dtype=jnp.int32)
    chosen_node = jnp.any(
        (expert_ids // 2)[:, :, None] == node_range[None, None, :], axis=1
    ).astype(jnp.float32)
    tok_range = jnp.arange(tok_count, dtype=jnp.int32)
    earlier = (tok_range[None, :] < tok_range[:, None]).astype(jnp.float32)
    node_rank = jnp.dot(earlier, chosen_node, precision=lax.Precision.HIGHEST)
    slot_range = jnp.arange(capacity, dtype=jnp.float32)
    dispatch = chosen_node[:, :, None] * (
        node_rank[:, :, None] == slot_range[None, None, :]
    ).astype(jnp.float32)
    outgoing = jnp.einsum(
        "tmc,td->mcd", dispatch.astype(jnp.bfloat16), tokens, preferred_element_type=jnp.float32
    ).astype(jnp.bfloat16)
    route_share = route_shares(affinity)
    pair_range = jnp.arange(2, dtype=jnp.int32)
    expert_grid = 2 * node_range[:, None] + pair_range[None, :]
    own_route = expert_ids[:, :, None, None] == expert_grid[None, None, :, :]
    pair_weight = jnp.sum(jnp.where(own_route, route_share[:, :, None, None], 0.0), axis=1)
    slot_weight = jnp.einsum(
        "tmc,tmp->mcp", dispatch, pair_weight, precision=lax.Precision.HIGHEST
    ).astype(jnp.bfloat16)
    arrived, arrived_weight = (
        lax.all_to_all(outgoing, "node", split_axis=0, concat_axis=0, tiled=True),
        lax.all_to_all(slot_weight, "node", split_axis=0, concat_axis=0, tiled=True),
    )
    expert_rows = arrived.reshape(node_count * capacity, half_width)
    gate_part = jnp.dot(expert_rows, w_gate[0], preferred_element_type=jnp.float32)
    up_part = jnp.dot(expert_rows, w_up[0], preferred_element_type=jnp.float32)
    gate_full, up_full = lax.psum((gate_part, up_part), "cuts")
    hidden = (jax.nn.silu(gate_full) * up_full).astype(jnp.bfloat16)
    slice_out = jnp.dot(hidden, w_down[0], preferred_element_type=jnp.float32)
    pick = (pair_range == pair_index).astype(jnp.float32)
    slot_scale = jnp.sum(arrived_weight.astype(jnp.float32) * pick[None, None, :], axis=2).reshape(
        node_count * capacity
    )
    weighted = (slice_out * slot_scale[:, None]).reshape(node_count, capacity, half_width)
    grouped = lax.psum_scatter(weighted, "local", scatter_dimension=2, tiled=True)
    returned = lax.all_to_all(grouped, "node", split_axis=0, concat_axis=0, tiled=True)
    partial_value = jnp.einsum("tmc,mcd->td", dispatch, returned, precision=lax.Precision.HIGHEST)
    summed = lax.all_to_all(partial_value, "local", split_axis=0, concat_axis=1, tiled=True)
    return summed.astype(jnp.bfloat16)


def on_device(tokens, expert_ids, affinity, w_gate, w_up, w_down):
    node_count = lax.axis_size("node")
    local_count = lax.axis_size("local")
    tok_count, top_count = expert_ids.shape
    expert_count = 2 * node_count
    capacity = (5 * tok_count * top_count + 4 * expert_count - 1) // (4 * expert_count)
    powers = all(size & (size - 1) == 0 for size in (node_count, local_count))
    everywhere = node_count == top_count // 2 and capacity >= tok_count and local_count * expert_count <= LANES
    everywhere = everywhere and node_count > 2 and local_count > 2
    chosen = dense_on_device if everywhere and powers and tok_count % local_count == 0 else slots_on_device
    return chosen(tokens, expert_ids, affinity, w_gate, w_up, w_down)


def solution(mesh):
    return jax.shard_map(
        on_device,
        mesh=mesh,
        in_specs=(
            P("node", "cuts"),
            P("node", None),
            P("node", None),
            P(("node", "local"), "cuts", None),
            P(("node", "local"), "cuts", None),
            P(("node", "local"), None, "cuts"),
        ),
        out_specs=P(("node", "local"), "cuts"),
        check_vma=False,
    )
```

```python
import jax
import jax.numpy as jnp
from jax import lax
from jax.experimental import pallas as pl
from jax.experimental.pallas import tpu as pltpu
from jax.sharding import PartitionSpec as P

LANES = 128


def swap(value, axis, bits):
    size = lax.axis_size(axis)
    return lax.ppermute(value, axis, [(i, i ^ bits) for i in range(size)])


def route_shares(affinity):
    affinity_sum = jnp.sum(affinity, axis=1, keepdims=True)
    return (2.5 * affinity / affinity_sum).astype(jnp.bfloat16).astype(jnp.float32)


def in_vmem(body, out_shapes, cost, *args):
    return pl.pallas_call(
        body,
        out_shape=out_shapes,
        in_specs=[pl.BlockSpec(memory_space=pltpu.VMEM)] * len(args),
        out_specs=jax.tree.map(lambda _: pl.BlockSpec(memory_space=pltpu.VMEM), out_shapes),
        compiler_params=pltpu.CompilerParams(vmem_limit_bytes=24 * 2**20),
        cost_estimate=pl.CostEstimate(flops=cost, bytes_accessed=2**20, transcendentals=0),
    )(*args)


def in_hbm(value):
    return pltpu.with_memory_space_constraint(value, pltpu.HBM)


def shape(*dims):
    return jax.ShapeDtypeStruct(dims, jnp.bfloat16)


def prepare(tokens, expert_ids, affinity, rows):
    tok_count, width = tokens.shape
    choices = expert_ids.shape[1]

    parts = tok_count // rows

    def body(tokens_hbm, ids_hbm, affinity_hbm, all_ref, share_ref, opposite_ref, ids_ref, affinity_ref, sems):
        copies = [
            pltpu.make_async_copy(tokens_hbm, all_ref.at[:, :width], sems.at[0]),
            pltpu.make_async_copy(ids_hbm, ids_ref, sems.at[1]),
            pltpu.make_async_copy(affinity_hbm, affinity_ref, sems.at[2]),
        ]
        for copy in copies:
            copy.start()
        copies[1].wait()
        copies[2].wait()
        total = jnp.sum(affinity_ref[...], axis=0, keepdims=True)
        share = (2.5 * affinity_ref[...] / total).astype(jnp.bfloat16).astype(jnp.float32)
        ids = ids_ref[...]
        lane = lax.broadcasted_iota(jnp.int32, (LANES, tok_count), 0)
        weight = jnp.zeros((LANES, tok_count), jnp.float32)
        for c in range(choices):
            weight += jnp.where(ids[c : c + 1, :] == lane, share[c : c + 1, :], 0.0)
        all_ref[:, width:] = weight.T.astype(jnp.bfloat16)
        copies[0].wait()
        for i in range(parts):
            other = i ^ (parts - 1)

            @pl.when(lax.axis_index("local") == i)
            def _():
                share_ref[...] = all_ref[i * rows : (i + 1) * rows, :]
                opposite_ref[...] = all_ref[other * rows : (other + 1) * rows, :]

    return pl.pallas_call(
        body,
        out_shape=(shape(tok_count, width + LANES), *[shape(rows, width + LANES)] * 2),
        in_specs=[pl.BlockSpec(memory_space=pltpu.HBM)] * 3,
        out_specs=[pl.BlockSpec(memory_space=pltpu.VMEM)] * 3,
        scratch_shapes=[
            pltpu.VMEM((choices, tok_count), jnp.int32),
            pltpu.VMEM((choices, tok_count), jnp.float32),
            pltpu.SemaphoreType.DMA((3,)),
        ],
        compiler_params=pltpu.CompilerParams(vmem_limit_bytes=24 * 2**20),
        cost_estimate=pl.CostEstimate(flops=10**6, bytes_accessed=2**20, transcendentals=0),
    )(*(in_hbm(value) for value in (tokens, expert_ids.T, affinity.T)))


def project_into(out_ref, rows, weight_refs, copies=()):
    hid = weight_refs[0].shape[1]
    for i, ref in enumerate(weight_refs):
        if copies:
            copies[i].wait()
        part = jnp.dot(rows, ref[...], preferred_element_type=jnp.float32)
        out_ref[:, i * hid : (i + 1) * hid] = part.astype(jnp.bfloat16)


def project(x, w_gate, w_up):
    count = x.shape[0]
    width, hid = w_gate.shape

    def body(x_ref, gate_ref, up_ref, out_ref):
        project_into(out_ref, x_ref[:, :width], (gate_ref, up_ref))

    return in_vmem(body, shape(count, 2 * hid), 4 * count * width * hid, x, w_gate, w_up)


def load_and_project(x, *weights):
    count = x.shape[0]
    width, hid = weights[0].shape

    def body(x_ref, gate_hbm, up_hbm, down_hbm, out_ref, gate_ref, up_ref, down_ref, sems):
        pairs = ((gate_hbm, gate_ref), (up_hbm, up_ref), (down_hbm, down_ref))
        copies = [pltpu.make_async_copy(src, dst, sems.at[i]) for i, (src, dst) in enumerate(pairs)]
        for copy in copies:
            copy.start()
        project_into(out_ref, x_ref[:, :width], (gate_ref, up_ref), copies)
        copies[2].wait()

    return pl.pallas_call(
        body,
        out_shape=(shape(count, 2 * hid), *(shape(*w.shape) for w in weights)),
        in_specs=[pl.BlockSpec(memory_space=pltpu.VMEM)] + [pl.BlockSpec(memory_space=pltpu.HBM)] * 3,
        out_specs=[pl.BlockSpec(memory_space=pltpu.VMEM)] * 4,
        scratch_shapes=[pltpu.SemaphoreType.DMA((3,))],
        compiler_params=pltpu.CompilerParams(vmem_limit_bytes=24 * 2**20),
    )(x, *(in_hbm(w) for w in weights))


def finish(x, part, other, w_down, group_size):
    count = x.shape[0]
    hid, width = w_down.shape

    def body(x_ref, part_ref, other_ref, down_ref, out_ref):
        both = part_ref[...].astype(jnp.float32) + other_ref[...].astype(jnp.float32)
        gate, up = both[:, :hid], both[:, hid:]
        hidden = (gate / (1.0 + jnp.exp(-gate)) * up).astype(jnp.bfloat16)
        expert = 2 * lax.axis_index("node") + lax.axis_index("local") // group_size
        lane = lax.broadcasted_iota(jnp.int32, (count, LANES), 1)
        table = x_ref[:, width:].astype(jnp.float32)
        scale = jnp.sum(jnp.where(lane == expert, table, 0.0), axis=1, keepdims=True)
        out = jnp.dot(hidden, down_ref[...], preferred_element_type=jnp.float32)
        out_ref[...] = (out * scale).astype(jnp.bfloat16)

    return in_vmem(body, shape(count, width), 2 * count * width * hid, x, part, other, w_down)


def merge(rows, partners, *values):
    count, width = values[0].shape
    parts = count // rows

    def body(own_ref, near_ref, direct_ref, *out_refs):
        for i in range(parts):

            @pl.when(lax.axis_index("local") == i)
            def _():
                for j, ref in zip((0, *partners), out_refs):
                    where = pl.ds((i ^ j) * rows, rows)
                    total = own_ref[where, :].astype(jnp.float32) + near_ref[where, :].astype(jnp.float32)
                    if j == parts - 1:
                        total += direct_ref[...].astype(jnp.float32)
                    ref[...] = total.astype(jnp.bfloat16)

    return in_vmem(body, tuple(shape(rows, width) for _ in range(parts)), 3 * count * width, *values)


def after(value, *others):
    return lax.optimization_barrier((value, *others))[0]


def dense_on_device(tokens, expert_ids, affinity, w_gate, w_up, w_down):
    node_count = lax.axis_size("node")
    local_count = lax.axis_size("local")
    group_size = local_count // 2
    tok_count, _ = expert_ids.shape
    rows = tok_count // local_count
    far = list(range(node_count - 1, 1, -1))

    def split(value):
        step = value.shape[0] // local_count
        return [value[j * step : (j + 1) * step] for j in range(local_count)]

    everything, own, opposite = prepare(tokens, expert_ids, affinity, rows)
    near = swap(everything, "node", 1)
    arrived = {k: swap(own, "node", k) for k in far}
    part_own, gate, up, down = load_and_project(everything, w_gate[0], w_up[0], w_down[0])

    def begin(x):
        part = project(x, gate, up)
        return x, part, swap(part, "cuts", 1)

    def complete(state, *others):
        x, part, other = state
        return finish(x, part, after(other, *others), down, group_size)

    sum_order = list(range(1, local_count))
    gather_order = sorted(sum_order, key=lambda j: (-j.bit_count(), j))

    def exchanged(blocks, order):
        return [swap(block, "local", j) for j, block in zip(order, blocks)]

    def summed(values):
        return sum(value.astype(jnp.float32) for value in values)

    arrived[far[0]] = after(arrived[far[0]], part_own)
    joined = jnp.concatenate([arrived[k] for k in far], axis=0)
    fewer = jnp.concatenate([arrived[k] for k in far[:-1]], axis=0)
    others = exchanged([fewer if j == local_count - 1 else joined for j in gather_order], gather_order)
    out_own = complete((everything, part_own, swap(part_own, "cuts", 1)))
    direct = swap(after(opposite, *arrived.values()), "node", far[-1])
    near_state = begin(near)
    out_near = complete(near_state)
    others[1] = after(others[1], near_state[1])
    others[2] = after(others[2], out_near)
    by_partner = [joined] + [others[gather_order.index(j)] for j in range(1, local_count)] + [direct]
    state = begin(after(jnp.concatenate(by_partner, axis=0), out_own))
    near_back = swap(out_near, "node", 1)
    out_far = complete(state, out_near)
    blocks = split(out_far)
    direct_back = swap(after(blocks[-1][-rows:], out_near), "node", far[-1])
    blocks[-1] = blocks[-1][:-rows]
    got = dict(zip(sum_order, exchanged([blocks[j] for j in sum_order], sum_order)))

    def piece(j, i):
        return got[j][i * rows : (i + 1) * rows]

    begun = summed([blocks[0][:-rows], got[local_count - 1]])
    rest = [j for j in sum_order if j != local_count - 1]
    begun, *values = lax.optimization_barrier((begun, *[got[j] for j in rest]))
    got.update(zip(rest, values))
    done = [begun[i * rows : (i + 1) * rows] for i in range(len(far) - 1)] + [blocks[0][-rows:].astype(jnp.float32)]
    done = [(value + summed([piece(j, i) for j in rest])).astype(jnp.bfloat16) for i, value in enumerate(done)]
    back = [swap(value, "node", k) for value, k in zip(done, far)]
    out_own = after(out_own, *done)
    mine, *blocks = merge(rows, gather_order, out_own, near_back, direct_back)
    later = exchanged(blocks, gather_order)
    total, *later = lax.optimization_barrier((summed(back), *later))
    return (total + summed([mine, *later])).astype(jnp.bfloat16)


def slots_on_device(tokens, expert_ids, affinity, w_gate, w_up, w_down):
    node_count = lax.axis_size("node")
    local_count = lax.axis_size("local")
    group_size = local_count // 2
    expert_count = 2 * node_count
    tok_count, top_count = expert_ids.shape
    capacity = (5 * tok_count * top_count + 4 * expert_count - 1) // (4 * expert_count)
    half_width = tokens.shape[1]
    my_local = lax.axis_index("local")
    pair_index = my_local // group_size
    node_range = jnp.arange(node_count, dtype=jnp.int32)
    chosen_node = jnp.any(
        (expert_ids // 2)[:, :, None] == node_range[None, None, :], axis=1
    ).astype(jnp.float32)
    tok_range = jnp.arange(tok_count, dtype=jnp.int32)
    earlier = (tok_range[None, :] < tok_range[:, None]).astype(jnp.float32)
    node_rank = jnp.dot(earlier, chosen_node, precision=lax.Precision.HIGHEST)
    slot_range = jnp.arange(capacity, dtype=jnp.float32)
    dispatch = chosen_node[:, :, None] * (
        node_rank[:, :, None] == slot_range[None, None, :]
    ).astype(jnp.float32)
    outgoing = jnp.einsum(
        "tmc,td->mcd", dispatch.astype(jnp.bfloat16), tokens, preferred_element_type=jnp.float32
    ).astype(jnp.bfloat16)
    route_share = route_shares(affinity)
    pair_range = jnp.arange(2, dtype=jnp.int32)
    expert_grid = 2 * node_range[:, None] + pair_range[None, :]
    own_route = expert_ids[:, :, None, None] == expert_grid[None, None, :, :]
    pair_weight = jnp.sum(jnp.where(own_route, route_share[:, :, None, None], 0.0), axis=1)
    slot_weight = jnp.einsum(
        "tmc,tmp->mcp", dispatch, pair_weight, precision=lax.Precision.HIGHEST
    ).astype(jnp.bfloat16)
    arrived, arrived_weight = (
        lax.all_to_all(outgoing, "node", split_axis=0, concat_axis=0, tiled=True),
        lax.all_to_all(slot_weight, "node", split_axis=0, concat_axis=0, tiled=True),
    )
    expert_rows = arrived.reshape(node_count * capacity, half_width)
    gate_part = jnp.dot(expert_rows, w_gate[0], preferred_element_type=jnp.float32)
    up_part = jnp.dot(expert_rows, w_up[0], preferred_element_type=jnp.float32)
    gate_full, up_full = lax.psum((gate_part, up_part), "cuts")
    hidden = (jax.nn.silu(gate_full) * up_full).astype(jnp.bfloat16)
    slice_out = jnp.dot(hidden, w_down[0], preferred_element_type=jnp.float32)
    pick = (pair_range == pair_index).astype(jnp.float32)
    slot_scale = jnp.sum(arrived_weight.astype(jnp.float32) * pick[None, None, :], axis=2).reshape(
        node_count * capacity
    )
    weighted = (slice_out * slot_scale[:, None]).reshape(node_count, capacity, half_width)
    grouped = lax.psum_scatter(weighted, "local", scatter_dimension=2, tiled=True)
    returned = lax.all_to_all(grouped, "node", split_axis=0, concat_axis=0, tiled=True)
    partial_value = jnp.einsum("tmc,mcd->td", dispatch, returned, precision=lax.Precision.HIGHEST)
    summed = lax.all_to_all(partial_value, "local", split_axis=0, concat_axis=1, tiled=True)
    return summed.astype(jnp.bfloat16)


def on_device(tokens, expert_ids, affinity, w_gate, w_up, w_down):
    node_count = lax.axis_size("node")
    local_count = lax.axis_size("local")
    tok_count, top_count = expert_ids.shape
    expert_count = 2 * node_count
    capacity = (5 * tok_count * top_count + 4 * expert_count - 1) // (4 * expert_count)
    powers = all(size & (size - 1) == 0 for size in (node_count, local_count))
    everywhere = node_count == top_count // 2 and capacity >= tok_count and expert_count <= LANES
    everywhere = everywhere and node_count > 2 and local_count > 2
    chosen = dense_on_device if everywhere and powers and tok_count % local_count == 0 else slots_on_device
    return chosen(tokens, expert_ids, affinity, w_gate, w_up, w_down)


def solution(mesh):
    return jax.shard_map(
        on_device,
        mesh=mesh,
        in_specs=(
            P("node", "cuts"),
            P("node", None),
            P("node", None),
            P(("node", "local"), "cuts", None),
            P(("node", "local"), "cuts", None),
            P(("node", "local"), None, "cuts"),
        ),
        out_specs=P(("node", "local"), "cuts"),
        check_vma=False,
    )
```
